256 devices in a mesh: rows: 64 (over x, y, z_hi), band: 4 (over z_lo, core).
Axes of the slice: x: 4, y: 4, z: 8 (z_hi: 4, z_lo: 2; z = z_hi * 2 + z_lo), core: 2. Of those that a mesh axis runs over, the one named last changes fastest.
Arguments:
- window: float32 [8, 1024, 8, 1024], P(None, 'rows', 'band'), may hold values from -8 to 8
- panels: float32 [3, 8, 1024, 1024], P(None, 'band', None, 'rows'), may hold values from -0.0625 to 0.0625
- inverse_gram: float32 [3, 1024, 1024], P(None, 'rows'), may hold values from -8 to 8
Outputs:
- final_window: float32 [8, 1024, 8, 1024], P(None, 'rows', 'band')
- finished: float32 [3, 1024, 1024], P(None, 'rows')
The draws below stay inside these ranges and needn't reach their ends.
All inputs are finite; a program needn't handle non-finite values.
Results may differ from the reference program's by a relative error of at most 0.0001.
Values sent between devices are 32-bit elements; how exact they have to be, the bound alone decides.
No kernel may reach another device: no remote copies, remote signals or barrier semaphores. Data moves between devices by JAX's collectives and lax.ppermute only.
A program may use at most 128 MiB of HBM per device.

```python
import jax
import jax.numpy as jnp
from jax import lax

B = 1024
W = 8
STEPS = 3


def steps_of(stream_key, dims, shards, smallest, largest):
    loudness = 1.0
    for axis_at, blocks in shards:
        steps = jax.random.uniform(jax.random.fold_in(jax.random.fold_in(stream_key, 6), axis_at), (blocks,), jnp.float32, smallest / len(shards), largest / len(shards))
        loudness = loudness * jnp.repeat(jnp.exp(steps), dims[axis_at] // blocks).reshape((-1,) + (1,) * (len(dims) - 1 - axis_at))
    return loudness


def noise(key, extent, deviation, bound, shards=(), kind=jnp.bfloat16):
    level = steps_of(key, extent, shards, -0.22, 0.18) if shards else 1.0
    result = jax.random.normal(key, extent, jnp.float32) * deviation * level
    return jnp.minimum(jnp.maximum(result, -bound), bound).astype(kind)


def setup_inputs(seed: int = 0) -> dict:
    key_of = jax.random.split(jax.random.key(seed), 4)
    return {
        "window": noise(key_of[0], (W, B, W, B), 1.0, 8.0, ((1, 64), (2, 4)), jnp.float32),
        "panels": noise(key_of[1], (STEPS, W, B, B), (W * B) ** -0.5, 0.0625, ((1, 4), (3, 64)), jnp.float32),
        "inverse_gram": noise(key_of[2], (STEPS, B, B), 1.0, 8.0, ((1, 64),), jnp.float32),
    }


def reference(window, panels, inverse_gram):
    full = W * B
    current = window.reshape(full, full)
    finished_list = []
    for section in range(STEPS):
        factor_now = panels[section].reshape(full, B)
        column = -jnp.dot(current, factor_now, precision=lax.Precision.HIGHEST, preferred_element_type=jnp.float32)
        diagonal = inverse_gram[section] - jnp.dot(column.T, factor_now, precision=lax.Precision.HIGHEST, preferred_element_type=jnp.float32)
        kept_tiles = column[: full - B]
        upper_rows = jnp.concatenate([diagonal, kept_tiles.T], axis=1)
        lower_rows = jnp.concatenate([kept_tiles, current[: full - B, : full - B]], axis=1)
        current = jnp.concatenate([upper_rows, lower_rows], axis=0)
        finished_list.append(column[full - B:])
    return current.reshape(W, B, W, B), jnp.stack(finished_list)
```

```python
import jax
import jax.numpy as jnp
from jax import lax
from jax.experimental import pallas as pl
from jax.experimental.pallas import tpu as pltpu
from jax.sharding import Mesh
from jax.sharding import PartitionSpec as P

RING = 4
BAND = ("zl", "core")
Q = ("y", "zh")
F32 = jnp.float32
VMEM_LIMIT = 30 * 1024 * 1024


def call(body, outs, here, *ins):
    return pl.pallas_call(
        body,
        out_shape=[jax.ShapeDtypeStruct(o, F32) for o in outs],
        in_specs=[pl.BlockSpec(memory_space=pltpu.SMEM)] + [pl.BlockSpec(memory_space=pltpu.VMEM)] * len(ins),
        out_specs=[pl.BlockSpec(memory_space=pltpu.VMEM)] * len(outs),
        compiler_params=pltpu.CompilerParams(vmem_limit_bytes=VMEM_LIMIT),
    )(here, *ins)


def split(x):
    high = x.astype(jnp.bfloat16)
    return high, (x - high.astype(F32)).astype(jnp.bfloat16)


def dot3(a, b):
    one = lambda p, q: lax.dot_general(p, q, (((1,), (1,)), ((), ())), preferred_element_type=F32)
    return one(a[0], b[0]) + (one(a[0], b[1]) + one(a[1], b[0]))


def nt(a, b):
    return dot3(split(a), split(b))


def forward(x, axis):
    return lax.ppermute(x, axis, [(i, (i + 1) % RING) for i in range(RING)])


def backward(x, axis):
    return lax.ppermute(x, axis, [(i, (i - 1) % RING) for i in range(RING)])


def swap(x, axis):
    return lax.ppermute(x, axis, [(0, 1), (1, 0)])


def band_move(x, pairs):
    return lax.ppermute(x, BAND, pairs)


def ring_gather(x, axis):
    half = x.shape[0] // 2
    behind = forward(x, axis)
    ahead = backward(x, axis)
    far_low = forward(behind[:half], axis)
    far_high = backward(ahead[half:], axis)
    return x, ahead, far_low, far_high, behind


def over_x(x):
    return lax.all_to_all(x, "x", 0, 0)


def over_q(x):
    return lax.all_to_all(x, Q, 0, 0)


def place(at, pieces, out):
    own, ahead, far_low, far_high, behind = pieces
    c = own.shape[1]
    half = own.shape[0] // 2
    for piece, first, offset in (
        (own, 0, 0), (ahead, 0, 1), (far_low, 0, 2), (far_high, half, 2), (behind, 0, 3)
    ):
        row = pl.multiple_of(lax.rem(at + offset, RING) * c, c)
        out[first : first + piece.shape[0], pl.ds(row, c), :] = piece[...]


def place_body(here, *refs):
    place(here[2], refs[:5], refs[5])


def window_product(here, pieces, v, kept, sent):
    own, ahead, far_low, far_high, behind = pieces
    total = None
    for b in range(2):
        far = (far_low, far_high)[b]
        rows = jnp.concatenate([own[b], ahead[b], far[0], behind[b]], axis=0)
        term = nt(rows, v[b])
        total = term if total is None else total + term
    core = here[4]
    block = own.shape[1]
    pair = block // 4
    for offset in range(RING):
        x = lax.rem(here[0] + offset, RING)
        for zl in range(2):
            for c in range(2):
                first = offset * block + (zl * 2 + c) * pair
                part = total[first : first + pair]

                @pl.when(core == c)
                def _():
                    kept[x, zl] = part

                @pl.when(core != c)
                def _():
                    sent[x, zl] = part


def first_product_body(here, *refs):
    v0 = refs[10]
    place(here[1], refs[5:10], v0)
    window_product(here, refs[:5], [v0[0], v0[1]], refs[11], refs[12])


def columns(ref, first):
    q, _, j, s = ref.shape
    return jnp.concatenate([ref[:, first + h].reshape(q * j, s) for h in range(2)], axis=1)


def later_product_body(here, *refs):
    batch = refs[5]
    window_product(here, refs[:5], [columns(batch, 0), columns(batch, 2)], refs[6], refs[7])


def middle_body(here, kept, got, kept2, sent2):
    zl = here[3]
    for z in range(2):
        part = kept[:, z] + got[:, z]

        @pl.when(zl == z)
        def _():
            kept2[...] = part

        @pl.when(zl != z)
        def _():
            sent2[...] = part


def edge(here, mine, other, n):
    q, _, j, s = mine.shape
    a = mine[:, n].reshape(q * j, s)
    b = other[:, n].reshape(q * j, s)
    first = here[4] == 0
    return jnp.concatenate([jnp.where(first, a, b), jnp.where(first, b, a)], axis=1)


def wide(ref):
    return jnp.concatenate([ref[x] for x in range(RING)], axis=1)


def blocks_of(kept, got):
    total = -(kept[...] + got[...])
    i = total.shape[1] // 2
    return jnp.concatenate([total[x, t * i : (t + 1) * i] for t in range(2) for x in range(RING)], axis=0)


def pack(u, out):
    half = u.shape[0] // 2
    turned = jnp.concatenate([u[:half].T, u[half:].T], axis=1)
    out[...] = turned.reshape(out.shape)


def repeat(value, out):
    for x in range(RING):
        out[x] = value


def column_body(here, kept, got, rep, packed):
    u = blocks_of(kept, got)
    repeat(u, rep)
    pack(u, packed)


def column_1_body(here, kept, got, u0_wide, e0, e0_other, rep, packed):
    u = blocks_of(kept, got) - nt(wide(u0_wide), edge(here, e0, e0_other, 0))
    repeat(u, rep)
    pack(u, packed)


def column_2_body(here, kept, got, u0_wide, u1_wide, e, e_other, by_row, packed):
    u = blocks_of(kept, got) - nt(wide(u1_wide), edge(here, e, e_other, 0))
    u = u - nt(wide(u0_wide), edge(here, e, e_other, 1))
    i = by_row.shape[2]
    for t in range(2):
        for x in range(RING):
            by_row[x, t] = u[(t * RING + x) * i : (t * RING + x + 1) * i]
    pack(u, packed)


def unpack_body(here, got, rep):
    q, j, lanes = got.shape
    i = lanes // 8
    for t in range(2):
        for x in range(RING):
            at = (t * RING + x) * i
            part = jnp.concatenate([got[d, :, at : at + i] for d in range(q)], axis=1)
            for r in range(RING):
                rep[r, t, :, x * q * i : (x + 1) * q * i] = part


def unpack_one_body(here, got, rep):
    q, j, lanes = got.shape
    i = lanes // 8
    for h in range(2):
        for x in range(RING):
            at = (h * RING + x) * i
            part = jnp.concatenate([got[d, :, at : at + i] for d in range(q)], axis=1)
            for r in range(RING):
                rep[r, h * j : (h + 1) * j, x * q * i : (x + 1) * q * i] = part


def tall(ref, t):
    x, _, j, s = ref.shape
    return ref[:, t].reshape(x * j, s)


def gram_first_body(here, turned, v0, b1, out):
    left = [split(tall(turned, t)) for t in range(2)]
    out[0] = sum(dot3(left[t], split(v0[t])) for t in range(2))
    out[1] = sum(dot3(left[t], split(columns(b1, 2 * t))) for t in range(2))


def gram_second_body(here, turned0, turned1, b1, b2, out):
    left0 = [split(tall(turned0, t)) for t in range(2)]
    left1 = [split(tall(turned1, t)) for t in range(2)]
    second = [split(columns(b2, 2 * t)) for t in range(2)]
    out[0] = sum(dot3(left1[t], split(columns(b1, 2 * t))) for t in range(2))
    out[1] = sum(dot3(left0[t], second[t]) for t in range(2))
    out[2] = sum(dot3(left1[t], second[t]) for t in range(2))


def gram_third_body(here, turned2, b2, out):
    out[...] = sum(nt(tall(turned2, t), columns(b2, 2 * t)) for t in range(2))


def gram_rows(gram, t):
    x, _, i, c = gram.shape
    return gram[:, t].reshape(x * i, c)


def d0_body(here, gram, m, m_got, rep):
    repeat(gram_rows(gram, 0) - (m[0] + m_got[0]), rep)


def x10_body(here, d0_wide, e0, e0_other, m, m_got, rep, packed):
    x10 = -(nt(wide(d0_wide), edge(here, e0, e0_other, 0)) + (m[1] + m_got[1]))
    repeat(x10, rep)
    q, j, lanes = packed.shape
    turned = x10.T.reshape(q, 2 * j, lanes // 2)
    packed[...] = jnp.concatenate([turned[:, :j], turned[:, j:]], axis=2)


def x21_body(here, d0_wide, x10_wide, e, e_other, m, m_got, out):
    out[...] = -(
        nt(wide(x10_wide), edge(here, e, e_other, 0))
        + nt(wide(d0_wide), edge(here, e, e_other, 1))
        + (m[1] + m_got[1])
    )


def turned_rows(ref):
    x, j, s = ref.shape
    return ref[...].reshape(x * j, s)


def d1_body(here, x10_t, e0, e0_other, gram, m, m_got, rep):
    d1 = gram_rows(gram, 1) - nt(turned_rows(x10_t), edge(here, e0, e0_other, 0)) - (m[0] + m_got[0])
    repeat(d1, rep)


def x20_body(here, d1_wide, x10_t, e, e_other, m, m_got, x21, x20, packed):
    x20[...] = -(
        nt(wide(d1_wide), edge(here, e, e_other, 0))
        + nt(turned_rows(x10_t), edge(here, e, e_other, 1))
        + (m[2] + m_got[2])
    )
    pack(jnp.concatenate([x20[...], x21[...]], axis=0), packed)


def d2_body(here, x2_t, e, e_other, gram, m, m_got, x20, x21, by_row):
    d2 = (
        gram_rows(gram, 2)
        - nt(tall(x2_t, 0), edge(here, e, e_other, 0))
        - nt(tall(x2_t, 1), edge(here, e, e_other, 1))
        - (m[...] + m_got[...])
    )
    i = by_row.shape[2]
    for n, value in enumerate((d2, x20[...], x21[...])):
        for x in range(RING):
            by_row[x, n] = value[x * i : (x + 1) * i]


def final_body(here, last, x2_t, x10_t, d0_wide, x10_wide, d1_wide, u01, u2, s_one, s_two, early_one, early_two, late_one, late_two, out):
    band = 2 * here[3] + here[4]
    i = out.shape[2]
    c = last.shape[3]

    def own(ref):
        at = pl.multiple_of(here[0] * i, i)
        return jnp.concatenate([ref[x, pl.ds(at, i), :] for x in range(RING)], axis=1)

    @pl.when(band == 0)
    def _():
        for x in range(RING):
            for n in range(3):
                out[0, n, :, x * c : (x + 1) * c] = last[x, n]
        out[1, 0] = x2_t[0]
        out[1, 1] = own(d1_wide)
        out[1, 2] = own(x10_wide)
        for a in range(5):
            out[0, 3 + a] = u2[a // 2, a % 2]
            out[1, 3 + a] = u01[a // 2, 1, a % 2]

    @pl.when(band == 1)
    def _():
        out[0, 0] = x2_t[1]
        out[0, 1] = x10_t[...]
        out[0, 2] = own(d0_wide)
        for a in range(5):
            out[0, 3 + a] = u01[a // 2, 0, a % 2]

    @pl.when(band >= 2)
    def _():
        out[0, 0] = late_two[...]
        out[0, 1:3] = early_two[...]
        out[0, 3:] = s_two[...]

    @pl.when(band >= 1)
    def _():
        out[1, 0] = late_one[...]
        out[1, 1:3] = early_one[...]
        out[1, 3:] = s_one[...]


def local(window, panels, inverse_gram):
    tiles, rows, cols, order = window.shape
    core = lax.axis_index("core")
    zl = lax.axis_index("zl")
    here = jnp.stack([lax.axis_index(a) for a in ("x", "y", "zh", "zl", "core")]).astype(jnp.int32)
    half = order // 2
    quarter = order // RING
    wide_rows = RING * rows
    q = RING * RING
    shards = jnp.transpose(panels, (0, 1, 3, 2))

    v0_part = call(place_body, [(cols, wide_rows, order)], here, *ring_gather(shards[0], "zh"))[0]
    v0_pieces = ring_gather(v0_part, "y")

    later = jnp.stack([shards[1, 0], shards[2, 0], shards[2, 1]])
    moved = band_move(later, [(1, 0), (2, 1), (3, 2)])
    low, high = later[:, :, :half], later[:, :, half:]
    edges = jnp.where(core == 0, low, lax.ppermute(high, "core", [(0, 1)]))
    edges = jnp.where(zl == 0, edges, lax.ppermute(edges, "zl", [(0, 1)]))
    halves = lambda p: [p[:, :half], p[:, half:]]
    batch_1 = jnp.stack(halves(shards[1, 1]) + halves(moved[0]) + [edges[0]])
    batch_2 = jnp.stack(halves(moved[1]) + halves(moved[2]) + [edges[1], edges[2]])
    batch_1 = lax.all_gather(batch_1, Q)
    batch_2 = lax.all_gather(batch_2, Q)

    window_b = jnp.transpose(window, (2, 0, 1, 3))
    s_pieces = ring_gather(window_b.reshape(cols, tiles * rows, order), "x")

    grams = jnp.transpose(inverse_gram.reshape(3, rows, RING, quarter), (2, 0, 1, 3))
    grams = over_x(grams)

    parts = (RING, 2, cols * rows, quarter)

    def scatter(kept, sent):
        kept, sent = call(middle_body, [(RING,) + parts[2:]] * 2, here, kept, swap(sent, "core"))
        return kept, swap(sent, "zl")

    block = (cols * wide_rows, quarter)
    rep = (RING,) + block
    packed = (q, rows, 2 * wide_rows)
    turned_rep = (RING, cols, rows, order)

    v0, kept, sent = call(
        first_product_body, [(cols, quarter, order), parts, parts], here, *s_pieces, *v0_pieces
    )
    u0, u0_packed = call(column_body, [rep, packed], here, *scatter(kept, sent))
    u0_wide = over_x(u0)
    u0_turned = call(unpack_body, [turned_rep], here, over_q(u0_packed))[0]
    u0_tall = over_x(u0_turned)

    e0 = batch_1[:, 4:]
    e0_other = swap(e0, "core")
    kept, sent = call(later_product_body, [parts, parts], here, *s_pieces, batch_1)
    u1, u1_packed = call(column_1_body, [rep, packed], here, *scatter(kept, sent), u0_wide, e0, e0_other)
    u1_wide = over_x(u1)
    u1_turned = call(unpack_body, [turned_rep], here, over_q(u1_packed))[0]
    u1_tall = over_x(u1_turned)

    m_first = call(gram_first_body, [(2, wide_rows, quarter)], here, u0_tall, v0, batch_1)[0]
    m_first = m_first + swap(m_first, "core")
    m_first = (m_first, swap(m_first, "zl"))

    e = batch_2[:, 4:]
    e_other = swap(e, "core")
    kept, sent = call(later_product_body, [parts, parts], here, *s_pieces, batch_2)
    u2, u2_packed = call(
        column_2_body, [(RING, cols, rows, quarter), packed], here, *scatter(kept, sent), u0_wide, u1_wide, e, e_other
    )
    u2_rows = over_x(u2)
    u2_turned = call(unpack_body, [turned_rep], here, over_q(u2_packed))[0]
    u2_tall = over_x(u2_turned)

    m_second = call(gram_second_body, [(3, wide_rows, quarter)], here, u0_tall, u1_tall, batch_1, batch_2)[0]
    m_second = m_second + swap(m_second, "core")
    m_second = (m_second, swap(m_second, "zl"))
    m_third = call(gram_third_body, [(wide_rows, quarter)], here, u2_tall, batch_2)[0]
    m_third = m_third + swap(m_third, "core")
    m_third = (m_third, swap(m_third, "zl"))

    small = (wide_rows, quarter)
    small_rep = (RING,) + small
    d0_wide = over_x(call(d0_body, [small_rep], here, grams, *m_first)[0])
    x10, x10_packed = call(
        x10_body, [small_rep, (q, rows // 2, 2 * wide_rows)], here, d0_wide, e0, e0_other, *m_first
    )
    x10_wide = over_x(x10)
    x10_turned = call(unpack_one_body, [(RING, rows, order)], here, over_q(x10_packed))[0]
    x10_t = over_x(x10_turned)
    x21 = call(x21_body, [small], here, d0_wide, x10_wide, e, e_other, *m_second)[0]
    d1_wide = over_x(call(d1_body, [small_rep], here, x10_t, e0, e0_other, grams, *m_second)[0])
    x20, x2_packed = call(x20_body, [small, packed], here, d1_wide, x10_t, e, e_other, *m_second, x21)
    x2_turned = call(unpack_body, [turned_rep], here, over_q(x2_packed))[0]
    x2_t = over_x(x2_turned)
    last = call(
        d2_body, [(RING, 3, rows, quarter)], here, x2_t, e, e_other, grams, *m_third, x20, x21
    )[0]
    last = over_x(last)

    one, two = [(0, 1), (1, 2), (2, 3)], [(0, 2), (1, 3)]
    kept_tiles = tiles - 3
    s_one = band_move(window_b[0, :kept_tiles], one)
    s_two = band_move(window_b[1, :kept_tiles], two)
    early = jnp.stack([u1_turned[0], u0_turned[0]])
    early_one, early_two = band_move(early[:, 0], one), band_move(early[:, 1], two)
    late_one, late_two = band_move(u2_turned[0, 0], one), band_move(u2_turned[0, 1], two)

    def own_rows(w):
        picked = lax.dynamic_slice_in_dim(w.reshape(RING, cols, RING, rows, quarter), here[0], 1, 2)
        return jnp.transpose(picked[:, :, 0], (1, 2, 0, 3)).reshape(cols, rows, order)

    u01_all = lax.all_gather(jnp.stack([own_rows(u0_wide), own_rows(u1_wide)]), BAND)
    u2_rows = jnp.transpose(u2_rows, (1, 2, 0, 3)).reshape(cols, rows, order)
    u2_all = lax.all_gather(u2_rows, BAND)

    final = call(
        final_body, [(cols, tiles, rows, order)], here,
        last, x2_turned[0], x10_turned[0], d0_wide, x10_wide, d1_wide, u01_all, u2_all,
        s_one, s_two, early_one, early_two, late_one, late_two,
    )[0]
    finished = jnp.stack([u01_all[3, 0, 1], u01_all[3, 1, 0], u2_all[2, 1]])
    return jnp.transpose(final, (1, 2, 0, 3)), finished


def solution(mesh):
    fine = Mesh(mesh.devices.reshape(RING, RING, RING, 2, 2), ("x", "y", "zh", "zl", "core"))
    rows = ("x", "y", "zh")
    return jax.shard_map(
        local,
        mesh=fine,
        in_specs=(P(None, rows, BAND, None), P(None, BAND, None, rows), P(None, rows, None)),
        out_specs=(P(None, rows, BAND, None), P(None, rows, None)),
        check_vma=False,
    )
```

```python
import functools

import jax
import jax.numpy as jnp
from jax import lax
from jax.experimental import pallas as pl
from jax.experimental.pallas import tpu as pltpu
from jax.sharding import Mesh
from jax.sharding import PartitionSpec as P

RING = 4
BAND = ("zl", "core")
Q = ("y", "zh")
F32 = jnp.float32
MIB = 1024 * 1024
A0_MIB = 16
A12_MIB = 24


def call(body, outs, here, *ins, wait=(), mib=8):
    leaves, tree = jax.tree.flatten(ins)
    n, m = len(leaves), len(wait)

    def run(here_ref, *refs):
        body(here_ref, *jax.tree.unflatten(tree, refs[:n]), *refs[n + m :])

    return pl.pallas_call(
        run,
        out_shape=[jax.ShapeDtypeStruct(o, F32) for o in outs],
        in_specs=[pl.BlockSpec(memory_space=pltpu.SMEM)]
        + [pl.BlockSpec(memory_space=pltpu.VMEM)] * n
        + [pl.BlockSpec(memory_space=pl.ANY)] * m,
        out_specs=[pl.BlockSpec(memory_space=pltpu.VMEM)] * len(outs),
        compiler_params=pltpu.CompilerParams(vmem_limit_bytes=mib * MIB),
    )(here, *leaves, *wait)


def split(x):
    high = x.astype(jnp.bfloat16)
    return high, (x - high.astype(F32)).astype(jnp.bfloat16)


def dot3(a, b):
    one = lambda p, q: lax.dot_general(p, q, (((1,), (1,)), ((), ())), preferred_element_type=F32)
    return one(a[0], b[0]) + (one(a[0], b[1]) + one(a[1], b[0]))


def nt(a, b):
    return dot3(split(a), split(b))


def forward(x, axis):
    return lax.ppermute(x, axis, [(i, (i + 1) % RING) for i in range(RING)])


def backward(x, axis):
    return lax.ppermute(x, axis, [(i, (i - 1) % RING) for i in range(RING)])


def swap(x, axis):
    return lax.ppermute(x, axis, [(0, 1), (1, 0)])


def band_move(x, pairs):
    return lax.ppermute(x, BAND, pairs)


def ring_gather(x, axis, halves=None):
    half = x.shape[0] // 2
    behind = forward(x, axis)
    ahead = backward(x, axis)
    low, high = halves(behind, ahead) if halves else (behind[:half], ahead[half:])
    return x, ahead, forward(low, axis), backward(high, axis), behind


def gather_x(x):
    return (x,) + tuple(
        lax.ppermute(x, "x", [((i + offset) % RING, i) for i in range(RING)]) for offset in range(1, RING)
    )


def spread_x(blocks):
    return (blocks[0],) + tuple(
        lax.ppermute(blocks[offset], "x", [(i, (i + offset) % RING) for i in range(RING)])
        for offset in range(1, RING)
    )


def over_q(x):
    return lax.all_to_all(x, Q, 0, 0)


def place(at, pieces, put):
    own, ahead, far_low, far_high, behind = pieces
    c = own.shape[1]
    half = own.shape[0] // 2
    for piece, first, offset in (
        (own, 0, 0), (ahead, 0, 1), (far_low, 0, 2), (far_high, half, 2), (behind, 0, 3)
    ):
        put(piece, first, pl.ds(pl.multiple_of(lax.rem(at + offset, RING) * c, c), c))


def place_body(here, pieces, out):
    def put(piece, first, rows):
        out[first : first + piece.shape[0], rows, :] = piece[...]

    place(here[2], pieces, put)


def batch_body(here, near, moved, edges, out):
    half = near.shape[1] // 2
    for n, tile in enumerate((near[...], moved[0], moved[1], moved[2])):
        out[2 * n] = tile[:, :half]
        out[2 * n + 1] = tile[:, half:]
    out[8:] = edges[...]


def window_product(here, pieces, steps, kept, sent):
    own, ahead, far_low, far_high, behind = pieces
    left = [split(jnp.concatenate([own[b], ahead[b], far[0], behind[b]], axis=0)) for b, far in enumerate((far_low, far_high))]
    core = here[4]
    block = own.shape[1]
    pair = block // 4
    for n, v in enumerate(steps):
        total = dot3(left[0], split(v[0])) + dot3(left[1], split(v[1]))
        for offset in range(RING):
            x = lax.rem(here[0] + offset, RING)
            for zl in range(2):
                for c in range(2):
                    first = offset * block + (zl * 2 + c) * pair
                    part = total[first : first + pair]

                    @pl.when(core == c)
                    def _():
                        kept[x, zl, n] = part

                    @pl.when(core != c)
                    def _():
                        sent[x, zl, n] = part


def first_product_body(here, s_pieces, v_pieces, v0, kept, sent):
    def put(piece, first, rows):
        v0[first : first + piece.shape[0], rows, :] = piece[...]

    place(here[1], v_pieces, put)
    window_product(here, s_pieces, [(v0[0], v0[1])], kept, sent)


def columns(v, first):
    return jnp.concatenate([v[first], v[first + 1]], axis=1)


def later_product_body(here, s_pieces, v_pieces, v12, e, kept, sent):
    n = v12.shape[0]

    def put(piece, first, rows):
        for m in range(piece.shape[0]):
            if first + m < n:
                v12[first + m, rows, :] = piece[m]
            else:
                e[first + m - n, rows, :] = piece[m]

    place(here[1], v_pieces, put)
    steps = [(columns(v12, 0), columns(v12, 2)), (columns(v12, 4), columns(v12, 6))]
    window_product(here, s_pieces, steps, kept, sent)


def halves_body(here, behind, ahead, low, high):
    half = low.shape[0]
    low[...] = behind[:half]
    high[...] = ahead[half:]


def middle_body(here, kept, got, kept2, sent2):
    zl = here[3]
    for z in range(2):
        part = kept[:, z] + got[:, z]

        @pl.when(zl == z)
        def _():
            kept2[...] = part

        @pl.when(zl != z)
        def _():
            sent2[...] = part


def edge(here, mine, other, n):
    first = here[4] == 0
    a, b = mine[n], other[n]
    return jnp.concatenate([jnp.where(first, a, b), jnp.where(first, b, a)], axis=1)


def join_columns(here, pieces, out):
    c = pieces[0].shape[1]
    for offset, piece in enumerate(pieces):
        x = lax.rem(here[0] + offset, RING)
        out[:, pl.ds(pl.multiple_of(x * c, c), c)] = piece[...]


def join_rows(here, pieces, out):
    j = pieces[0].shape[-2]
    for offset, piece in enumerate(pieces):
        x = lax.rem(here[0] + offset, RING)
        rows = pl.ds(pl.multiple_of(x * j, j), j)
        if len(out.shape) == 2:
            out[rows, :] = piece[...]
        else:
            out[:, rows, :] = piece[...]


def blocks_of(kept, got, n):
    total = -(kept[:, n] + got[:, n])
    i = total.shape[1] // 2
    return jnp.concatenate([total[x, t * i : (t + 1) * i] for t in range(2) for x in range(RING)], axis=0)


def pack(blocks, out):
    q = out.shape[0]
    for n, u in enumerate(blocks):
        half = u.shape[0] // 2
        turned = jnp.concatenate([u[:half].T, u[half:].T], axis=1)
        j = turned.shape[0] // q
        out[:, n * j : (n + 1) * j, :] = turned.reshape(q, j, 2 * half)


def ahead_of(here, offset):
    return lax.rem(here[0] + offset, RING)


def behind(here, offset):
    return lax.rem(here[0] + RING - offset, RING)


def by_offset(here, u, outs):
    for offset, out in enumerate(outs):
        t, i, _ = out.shape
        for n in range(t):
            at = pl.multiple_of(n * RING * i + ahead_of(here, offset) * i, i)
            out[n] = u[pl.ds(at, i), :]


def put_columns(here, pieces, n, put):
    for offset, piece in enumerate(pieces):
        c = piece.shape[2]
        put(pl.ds(pl.multiple_of(behind(here, offset) * c, c), c), piece[n])


def column_0_body(here, kept, got, u0, packed):
    u0[...] = blocks_of(kept, got, 0)
    pack([u0[...]], packed)


def column_1_body(here, kept, got, u0_pieces, e, e_other, u1, u0_wide):
    join_columns(here, u0_pieces, u0_wide)
    u1[...] = blocks_of(kept, got, 0) - nt(u0_wide[...], edge(here, e, e_other, 0))


def column_2_body(here, kept, got, u0_wide, u1_pieces, e, e_other, x10, u1_wide, packed, u2):
    join_columns(here, u1_pieces, u1_wide)
    later = blocks_of(kept, got, 1) - nt(u1_wide[...], edge(here, e, e_other, 1))
    u2[...] = later - nt(u0_wide[...], edge(here, e, e_other, 2))
    j = x10.shape[1] // packed.shape[0]
    pack([u1_pieces[0][...], u2[...]], packed.at[:, : 2 * j])
    q = packed.shape[0]
    turned = x10[...].T.reshape(q, j, x10.shape[0])
    packed[:, 2 * j :] = jnp.concatenate([turned[:, : j // 2], turned[:, j // 2 :]], axis=2)


def by_offset_body(here, u, *outs):
    by_offset(here, u, outs)


def unpack_body(here, got, out):
    q, rows, lanes = got.shape
    i = lanes // 8
    j = out.shape[1]
    for n in range(rows // j):
        for t in range(2):
            for x in range(RING):
                at = (t * RING + x) * i
                out[2 * n + t, :, x * q * i : (x + 1) * q * i] = jnp.concatenate(
                    [got[d, n * j : (n + 1) * j, at : at + i] for d in range(q)], axis=1
                )


def unpack_more_body(here, got, out):
    q, _, lanes = got.shape
    i = lanes // 8
    j = out.shape[1]
    for n in range(3):
        rows = slice(n * j, n * j + (j if n < 2 else j // 2))
        for h in range(2):
            for x in range(RING):
                at = (h * RING + x) * i
                part = jnp.concatenate([got[d, rows, at : at + i] for d in range(q)], axis=1)
                columns_x = slice(x * q * i, (x + 1) * q * i)
                if n < 2:
                    out[2 * n + h, :, columns_x] = part
                else:
                    out[4, h * (j // 2) : (h + 1) * (j // 2), columns_x] = part


def gram_00_body(here, pieces, v0, out, tall0):
    join_rows(here, pieces, tall0)
    out[...] = sum(nt(tall0[t], v0[t]) for t in range(2))


def gram_01_body(here, tall0, v12, out):
    out[...] = sum(nt(tall0[t], columns(v12, 2 * t)) for t in range(2))


def gram_second_body(here, tall0, pieces, v12, out, tall12):
    join_rows(here, pieces, tall12)
    left = [[split(t) for t in tiles] for tiles in ((tall0[0], tall0[1]), (tall12[0], tall12[1]), (tall12[2], tall12[3]))]
    v1 = [split(columns(v12, 2 * t)) for t in range(2)]
    v2 = [split(columns(v12, 4 + 2 * t)) for t in range(2)]
    for n, (a, v) in enumerate(((1, v1), (0, v2), (1, v2), (2, v2))):
        out[n] = sum(dot3(left[a][t], v[t]) for t in range(2))


def gram_body(here, gram, *outs):
    for offset, out in enumerate(outs):
        c = out.shape[2]
        out[...] = gram[:, :, pl.ds(pl.multiple_of(ahead_of(here, offset) * c, c), c)]


def d0_body(here, gram_pieces, m, m_got, d0, gram):
    for offset, piece in enumerate(gram_pieces):
        i = piece.shape[1]
        gram[:, pl.ds(pl.multiple_of(behind(here, offset) * i, i), i), :] = piece[...]
    d0[...] = gram[0] - (m[...] + m_got[...])


def x10_body(here, d0_pieces, e, e_other, m, m_got, x10, d0_wide):
    join_columns(here, d0_pieces, d0_wide)
    x10[...] = -(nt(d0_wide[...], edge(here, e, e_other, 0)) + (m[...] + m_got[...]))


def d1_body(here, x10_t, e, e_other, gram, m, m_got, d1):
    d1[...] = gram[1] - nt(x10_t[4], edge(here, e, e_other, 0)) - (m[0] + m_got[0])


def x2_body(here, d0_wide, x10_pieces, d1_pieces, x10_t, e, e_other, m, m_got, packed, x2, x10_wide, d1_wide):
    join_columns(here, x10_pieces, x10_wide)
    join_columns(here, d1_pieces, d1_wide)
    e1, e2 = split(edge(here, e, e_other, 1)), split(edge(here, e, e_other, 2))
    x20 = -(dot3(split(d1_wide[...]), e1) + dot3(split(x10_t[4]), e2) + (m[2] + m_got[2]))
    x21 = -(dot3(split(x10_wide[...]), e1) + dot3(split(d0_wide[...]), e2) + (m[1] + m_got[1]))
    x2[...] = jnp.concatenate([x20, x21], axis=0)
    pack([x2[...]], packed)


def d2_body(here, x2_t_pieces, e, e_other, gram, m, m_got, x2, x2_t, new, *outs):
    join_rows(here, x2_t_pieces, x2_t)
    n = gram.shape[1]
    new[n:] = x2[...]
    new[:n] = (
        gram[2]
        - nt(x2_t[0], edge(here, e, e_other, 1))
        - nt(x2_t[1], edge(here, e, e_other, 2))
        - (m[3] + m_got[3])
    )
    by_offset(here, new, outs)


def corner_body(here, pieces, x2_turned, turned12, d0_wide, slot_0, slot_1):
    band = 2 * here[3] + here[4]
    i = slot_0.shape[1]

    @pl.when(band == 0)
    def _():
        def put(n, at, value):
            slot_0[n, :, at] = value

        for n in range(3):
            put_columns(here, pieces, n, functools.partial(put, n))

    @pl.when(band != 0)
    def _():
        slot_0[0] = x2_turned[1]
        slot_0[1] = turned12[4]
        slot_0[2] = d0_wide[pl.ds(pl.multiple_of(here[0] * i, i), i), :]

    slot_1[...] = x2_turned[0]


def payload_body(here, u0, u1, u2, turned0, turned12, out):
    i = out.shape[2]
    at = pl.multiple_of(here[0] * i, i)

    def put(t, columns_x, value):
        out[2, t, :, columns_x] = value

    for t in range(2):
        for n, ref in enumerate((u0, u1)):
            out[n, t] = ref[pl.ds(t * RING * i + at, i), :]
        put_columns(here, u2, t, functools.partial(put, t))
        out[3, t] = turned0[t]
        out[4, t] = turned12[t]
        out[5, t] = turned12[2 + t]


def final_body(here, x10_wide, d1_wide, shared, s_one, s_two, out, done):
    band = 2 * here[3] + here[4]
    i = out.shape[2]
    own = pl.ds(pl.multiple_of(here[0] * i, i), i)
    done[0] = shared[3, 0, 1]
    done[1] = shared[3, 1, 0]
    done[2] = shared[2, 2, 1]

    @pl.when(band == 0)
    def _():
        out[0, :3] = jnp.zeros((3,) + out.shape[2:], out.dtype)
        out[1, 0] = jnp.zeros(out.shape[2:], out.dtype)
        out[1, 1] = d1_wide[own, :]
        out[1, 2] = x10_wide[own, :]
        for a in range(5):
            out[0, 3 + a] = shared[a // 2, 2, a % 2]
            out[1, 3 + a] = shared[a // 2, 1, a % 2]

    @pl.when(band == 1)
    def _():
        out[0, :3] = jnp.zeros((3,) + out.shape[2:], out.dtype)
        for a in range(5):
            out[0, 3 + a] = shared[a // 2, 0, a % 2]

    @pl.when(band >= 2)
    def _():
        for a in range(3):
            out[0, a] = shared[band - 2, 5 - a, 1]
        out[0, 3:] = s_two[...]

    @pl.when(band >= 1)
    def _():
        for a in range(3):
            out[1, a] = shared[band - 1, 5 - a, 0]
        out[1, 3:] = s_one[...]


def local(window, panels, inverse_gram):
    tiles, rows, cols, order = window.shape
    core = lax.axis_index("core")
    zl = lax.axis_index("zl")
    here = jnp.stack([lax.axis_index(a) for a in ("x", "y", "zh", "zl", "core")]).astype(jnp.int32)
    half = order // 2
    quarter = order // RING
    wide_rows = RING * rows
    q = RING * RING
    shards = jnp.transpose(panels, (0, 1, 3, 2))

    v0_zh = ring_gather(shards[0], "zh")
    window_b = jnp.transpose(window, (2, 0, 1, 3))
    s_pieces = ring_gather(window_b.reshape(cols, tiles * rows, order), "x")
    v0_part = call(place_body, [(cols, wide_rows, order)], here, v0_zh)[0]
    v0_pieces = ring_gather(v0_part, "y")

    later = jnp.stack([shards[1, 0], shards[2, 0], shards[2, 1]])
    moved = band_move(later, [(1, 0), (2, 1), (3, 2)])
    low, high = later[:, :, :half], later[:, :, half:]
    edges = jnp.where(core == 0, low, lax.ppermute(high, "core", [(0, 1)]))
    edges = jnp.where(zl == 0, edges, lax.ppermute(edges, "zl", [(0, 1)]))
    batch = call(batch_body, [(11, rows, half)], here, shards[1, 1], moved, edges, wait=(v0_part, s_pieces[1], s_pieces[4]))[0]

    def batch_halves(wait):
        def cut(behind, ahead):
            n, c, s = behind.shape
            return call(halves_body, [(n // 2, c, s), (n - n // 2, c, s)], here, behind, ahead, wait=wait)

        return cut

    batch_zh = ring_gather(batch, "zh", batch_halves((v0_pieces[1], v0_pieces[4], s_pieces[2], s_pieces[3])))

    gram_pieces = spread_x(call(gram_body, [(3, rows, quarter)] * RING, here, inverse_gram))

    def scatter(kept, sent):
        kept, sent = call(middle_body, [kept.shape[:1] + kept.shape[2:]] * 2, here, kept, swap(sent, "core"))
        return kept, swap(sent, "zl")

    def parts(n):
        return (RING, 2, n, cols * rows, quarter)

    block = (cols * wide_rows, quarter)
    wide = (cols * wide_rows, order)

    v0, kept, sent = call(
        first_product_body, [(cols, quarter, order), parts(1), parts(1)], here, s_pieces, v0_pieces,
        wait=gram_pieces[1:], mib=A0_MIB,
    )
    batch_part = call(place_body, [(11, wide_rows, half)], here, batch_zh, wait=(v0_pieces[2], v0_pieces[3]))[0]
    u0, u0_packed = call(column_0_body, [block, (q, rows, cols * wide_rows)], here, *scatter(kept, sent))
    u0_turned = call(unpack_body, [(cols, rows, order)], here, over_q(u0_packed))[0]
    batch_pieces = ring_gather(batch_part, "y", batch_halves((u0_turned,)))
    u0_pieces = gather_x(u0)
    tall0_pieces = gather_x(u0_turned)

    def band_sum(m):
        m = m + swap(m, "core")
        return m, swap(m, "zl")

    small = (wide_rows, quarter)
    m_00, tall0 = call(
        gram_00_body, [small, (cols, wide_rows, order)], here, tall0_pieces, v0, mib=16
    )
    d0, gram = call(d0_body, [small, (3,) + small], here, gram_pieces, *band_sum(m_00))
    d0_pieces = gather_x(d0)

    v12, e, kept, sent = call(
        later_product_body,
        [(8, quarter, half), (3, quarter, half), parts(2), parts(2)], here, s_pieces, batch_pieces, wait=d0_pieces[1:], mib=A12_MIB,
    )
    e_other = swap(e, "core")
    kept, got = scatter(kept, sent)
    u1, u0_wide = call(column_1_body, [block, wide], here, kept, got, u0_pieces, e, e_other)
    m_01 = call(gram_01_body, [small], here, tall0, v12, mib=16)[0]
    m_01 = band_sum(m_01)
    x10, d0_wide = call(x10_body, [small, (wide_rows, order)], here, d0_pieces, e, e_other, *m_01)
    by_rows = (cols, rows, quarter)
    u1_wide, packed, u2 = call(
        column_2_body,
        [wide, (q, 2 * rows + rows // 2, cols * wide_rows), block], here,
        kept, got, u0_wide, gather_x(u1), e, e_other, x10,
    )
    turned12 = call(unpack_more_body, [(5, rows, order)], here, over_q(packed))[0]
    m_second, tall12 = call(
        gram_second_body, [(4, wide_rows, quarter), (5, wide_rows, order)], here,
        tall0, gather_x(turned12), v12, mib=20,
    )
    m_second = band_sum(m_second)
    d1 = call(d1_body, [small], here, tall12, e, e_other, gram, *m_second)[0]
    x2_packed, x2, x10_wide, d1_wide = call(
        x2_body,
        [(q, rows, cols * wide_rows), block, (wide_rows, order), (wide_rows, order)], here,
        d0_wide, gather_x(x10), gather_x(d1), tall12, e, e_other, *m_second,
    )
    x2_turned = call(unpack_body, [(cols, rows, order)], here, over_q(x2_packed))[0]
    kept_tiles = tiles - 3
    s_one = band_move(window_b[0, :kept_tiles], [(0, 1), (1, 2), (2, 3)])
    s_two = band_move(window_b[1, :kept_tiles], [(0, 2), (1, 3)])
    u2_rows = spread_x(call(by_offset_body, [by_rows] * RING, here, u2, wait=(turned12,)))
    payload = call(
        payload_body, [(6, cols, rows, order)], here, u0_wide, u1_wide, u2_rows, u0_turned, turned12, wait=(d1,)
    )[0]
    shared = lax.all_gather(payload, BAND)

    final, finished = call(
        final_body, [(cols, tiles, rows, order), (3, rows, order)], here, x10_wide, d1_wide, shared, s_one, s_two
    )
    final = jnp.transpose(final, (1, 2, 0, 3))
    _, _, *new = call(
        d2_body, [(cols, wide_rows, order), (3 * wide_rows, quarter)] + [(3, rows, quarter)] * RING, here,
        gather_x(x2_turned), e, e_other, gram, *m_second, x2,
    )
    slot_0, slot_1 = call(
        corner_body, [(3, rows, order), (rows, order)], here, spread_x(new), x2_turned, turned12, d0_wide,
        wait=(final,),
    )
    left = zl == 0
    final = final.at[:3, :, 0, :].set(jnp.where(left, slot_0, final[:3, :, 0, :]))
    final = final.at[0, :, 1, :].set(jnp.where(left & (core == 0), slot_1, final[0, :, 1, :]))
    return final, finished


def solution(mesh):
    fine = Mesh(mesh.devices.reshape(RING, RING, RING, 2, 2), ("x", "y", "zh", "zl", "core"))
    rows = ("x", "y", "zh")
    return jax.shard_map(
        local,
        mesh=fine,
        in_specs=(P(None, rows, BAND, None), P(None, BAND, None, rows), P(None, rows, None)),
        out_specs=(P(None, rows, BAND, None), P(None, rows, None)),
        check_vma=False,
    )
```

```python
import functools

import jax
import jax.numpy as jnp
from jax import lax
from jax.experimental import pallas as pl
from jax.experimental.pallas import tpu as pltpu
from jax.sharding import Mesh
from jax.sharding import PartitionSpec as P

RING = 4
BAND = ("zl", "core")
Q = ("y", "zh")
F32 = jnp.float32
MIB = 1024 * 1024
A0_MIB = 16
A12_MIB = 24


def call(body, outs, here, *ins, wait=(), mib=8, alias=None):
    leaves, tree = jax.tree.flatten(ins)
    n, m = len(leaves), len(wait)

    def run(here_ref, *refs):
        body(here_ref, *jax.tree.unflatten(tree, refs[:n]), *refs[n + m :])

    return pl.pallas_call(
        run,
        out_shape=[jax.ShapeDtypeStruct(o, F32) for o in outs],
        in_specs=[pl.BlockSpec(memory_space=pltpu.SMEM)]
        + [pl.BlockSpec(memory_space=pltpu.VMEM)] * n
        + [pl.BlockSpec(memory_space=pl.ANY)] * m,
        out_specs=[pl.BlockSpec(memory_space=pltpu.VMEM)] * len(outs),
        input_output_aliases=alias or {},
        compiler_params=pltpu.CompilerParams(vmem_limit_bytes=mib * MIB),
    )(here, *leaves, *wait)


def split(x):
    high = x.astype(jnp.bfloat16)
    return high, (x - high.astype(F32)).astype(jnp.bfloat16)


def dot3(a, b):
    one = lambda p, q: lax.dot_general(p, q, (((1,), (1,)), ((), ())), preferred_element_type=F32)
    return one(a[0], b[0]) + (one(a[0], b[1]) + one(a[1], b[0]))


def nt(a, b):
    return dot3(split(a), split(b))


def forward(x, axis):
    return lax.ppermute(x, axis, [(i, (i + 1) % RING) for i in range(RING)])


def backward(x, axis):
    return lax.ppermute(x, axis, [(i, (i - 1) % RING) for i in range(RING)])


def swap(x, axis):
    return lax.ppermute(x, axis, [(0, 1), (1, 0)])


def band_move(x, pairs):
    return lax.ppermute(x, BAND, pairs)


def ring_gather(x, axis, halves=None):
    half = x.shape[0] // 2
    behind = forward(x, axis)
    ahead = backward(x, axis)
    low, high = halves(behind, ahead) if halves else (behind[:half], ahead[half:])
    return x, ahead, forward(low, axis), backward(high, axis), behind


def gather_x(x):
    return (x,) + tuple(
        lax.ppermute(x, "x", [((i + offset) % RING, i) for i in range(RING)]) for offset in range(1, RING)
    )


def spread_x(blocks):
    return (blocks[0],) + tuple(
        lax.ppermute(blocks[offset], "x", [(i, (i + offset) % RING) for i in range(RING)])
        for offset in range(1, RING)
    )


def over_q(x):
    return lax.all_to_all(x, Q, 0, 0)


def place(at, pieces, put):
    own, ahead, far_low, far_high, behind = pieces
    c = own.shape[1]
    half = own.shape[0] // 2
    for piece, first, offset in (
        (own, 0, 0), (ahead, 0, 1), (far_low, 0, 2), (far_high, half, 2), (behind, 0, 3)
    ):
        put(piece, first, pl.ds(pl.multiple_of(lax.rem(at + offset, RING) * c, c), c))


def place_body(here, pieces, out):
    def put(piece, first, rows):
        out[first : first + piece.shape[0], rows, :] = piece[...]

    place(here[2], pieces, put)


def batch_body(here, near, moved, edges, out):
    half = near.shape[1] // 2
    for n, tile in enumerate((near[...], moved[0], moved[1], moved[2])):
        out[2 * n] = tile[:, :half]
        out[2 * n + 1] = tile[:, half:]
    out[8:] = edges[...]


def window_product(here, pieces, v, kept, sent):
    total = None
    for b in range(2):
        rows = jnp.concatenate([pieces[0][b], pieces[1][b], pieces[2 + b][0], pieces[4][b]], axis=0)
        term = nt(rows, v[b])
        total = term if total is None else total + term
    core = here[4]
    block = pieces[0].shape[1]
    pair = block // 4
    for offset in range(RING):
        x = ahead_of(here, offset)
        for zl in range(2):
            for c in range(2):
                first = offset * block + (zl * 2 + c) * pair
                part = total[first : first + pair]

                @pl.when(core == c)
                def _():
                    kept[x, zl] = part

                @pl.when(core != c)
                def _():
                    sent[x, zl] = part


def first_product_body(here, s_pieces, v_pieces, v0, kept, sent):
    def put(piece, first, rows):
        v0[first : first + piece.shape[0], rows, :] = piece[...]

    place(here[1], v_pieces, put)
    window_product(here, s_pieces, (v0[0], v0[1]), kept, sent)


def columns(v, first):
    return jnp.concatenate([v[first], v[first + 1]], axis=1)


def later_product_body(here, s_pieces, v_pieces, v12, e, kept, sent):
    n = v12.shape[0]

    def put(piece, first, rows):
        for m in range(piece.shape[0]):
            if first + m < n:
                v12[first + m, rows, :] = piece[m]
            else:
                e[first + m - n, rows, :] = piece[m]

    place(here[1], v_pieces, put)
    window_product(here, s_pieces, (columns(v12, 0), columns(v12, 2)), kept, sent)


def last_product_body(here, s_pieces, v12, kept, sent):
    window_product(here, s_pieces, (columns(v12, 4), columns(v12, 6)), kept, sent)


def halves_body(here, behind, ahead, low, high):
    half = low.shape[0]
    low[...] = behind[:half]
    high[...] = ahead[half:]


def middle_body(here, kept, got, kept2, sent2):
    zl = here[3]
    for z in range(2):
        part = kept[:, z] + got[:, z]

        @pl.when(zl == z)
        def _():
            kept2[...] = part

        @pl.when(zl != z)
        def _():
            sent2[...] = part


def edge(here, mine, other, n):
    first = here[4] == 0
    a, b = mine[n], other[n]
    return jnp.concatenate([jnp.where(first, a, b), jnp.where(first, b, a)], axis=1)


def join_columns(here, pieces, out):
    c = pieces[0].shape[1]
    for offset, piece in enumerate(pieces):
        x = lax.rem(here[0] + offset, RING)
        out[:, pl.ds(pl.multiple_of(x * c, c), c)] = piece[...]


def join_rows(here, pieces, out):
    j = pieces[0].shape[-2]
    for offset, piece in enumerate(pieces):
        x = lax.rem(here[0] + offset, RING)
        rows = pl.ds(pl.multiple_of(x * j, j), j)
        if len(out.shape) == 2:
            out[rows, :] = piece[...]
        else:
            out[:, rows, :] = piece[...]


def blocks_of(kept, got):
    total = -(kept[...] + got[...])
    i = total.shape[1] // 2
    return jnp.concatenate([total[x, t * i : (t + 1) * i] for t in range(2) for x in range(RING)], axis=0)


def pack(blocks, out):
    q = out.shape[0]
    for n, u in enumerate(blocks):
        half = u.shape[0] // 2
        turned = jnp.concatenate([u[:half].T, u[half:].T], axis=1)
        j = turned.shape[0] // q
        out[:, n * j : (n + 1) * j, :] = turned.reshape(q, j, 2 * half)


def ahead_of(here, offset):
    return lax.rem(here[0] + offset, RING)


def behind(here, offset):
    return lax.rem(here[0] + RING - offset, RING)


def by_offset(here, u, outs):
    for offset, out in enumerate(outs):
        t, i, _ = out.shape
        for n in range(t):
            at = pl.multiple_of(n * RING * i + ahead_of(here, offset) * i, i)
            out[n] = u[pl.ds(at, i), :]


def put_columns(here, pieces, n, put):
    for offset, piece in enumerate(pieces):
        c = piece.shape[2]
        put(pl.ds(pl.multiple_of(behind(here, offset) * c, c), c), piece[n])


def column_0_body(here, kept, got, u0, packed):
    u0[...] = blocks_of(kept, got)
    pack([u0[...]], packed)


def column_1_body(here, kept, got, u0_wide, e, e_other, d0, out):
    m = u0_wide.shape[0]
    out[:m] = blocks_of(kept, got) - nt(u0_wide[...], edge(here, e, e_other, 0))
    out[m:] = d0[...]


def column_2_body(here, kept, got, u0_wide, pieces, e, e_other, m, both_wide, packed, u2, x10):
    join_columns(here, pieces, both_wide)
    n = u2.shape[0]
    e0 = edge(here, e, e_other, 0)
    later = blocks_of(kept, got) - nt(both_wide[:n], edge(here, e, e_other, 1))
    u2[...] = later - nt(u0_wide[...], edge(here, e, e_other, 2))
    x10[...] = -(nt(both_wide[n:], e0) + sum_of(m))
    j = x10.shape[1] // packed.shape[0]
    pack([pieces[0][:n], u2[...]], packed.at[:, : 2 * j])
    q = packed.shape[0]
    turned = x10[...].T.reshape(q, j, x10.shape[0])
    packed[:, 2 * j :] = jnp.concatenate([turned[:, : j // 2], turned[:, j // 2 :]], axis=2)


def shift_body(here, window, one, two):
    n = one.shape[0]
    one[...] = window[0, :n]
    two[...] = window[1, :n]


def by_offset_body(here, u, *outs):
    by_offset(here, u, outs)


def unpack_body(here, got, out):
    q, rows, lanes = got.shape
    i = lanes // 8
    j = out.shape[1]
    for n in range(rows // j):
        for t in range(2):
            for x in range(RING):
                at = (t * RING + x) * i
                out[2 * n + t, :, x * q * i : (x + 1) * q * i] = jnp.concatenate(
                    [got[d, n * j : (n + 1) * j, at : at + i] for d in range(q)], axis=1
                )


def unpack_first_body(here, got, u0, turned, out):
    unpack_body(here, got, turned)
    n, j, _ = turned.shape
    m, c = u0.shape
    out[:m] = u0[...]
    for t in range(n):
        for x in range(RING):
            at = m + (t * RING + x) * j
            out[at : at + j] = turned[t, :, x * c : (x + 1) * c]


def unpack_more_body(here, got, out):
    q, _, lanes = got.shape
    i = lanes // 8
    j = out.shape[1]
    for n in range(3):
        rows = slice(n * j, n * j + (j if n < 2 else j // 2))
        for h in range(2):
            for x in range(RING):
                at = (h * RING + x) * i
                part = jnp.concatenate([got[d, rows, at : at + i] for d in range(q)], axis=1)
                columns_x = slice(x * q * i, (x + 1) * q * i)
                if n < 2:
                    out[2 * n + h, :, columns_x] = part
                else:
                    out[4, h * (j // 2) : (h + 1) * (j // 2), columns_x] = part


def gram_00_body(here, pieces, v0, out, tall0, u0_wide):
    n, wide_rows, _ = tall0.shape
    j = wide_rows // RING
    m, c = u0_wide.shape[0], pieces[0].shape[1]
    for offset, piece in enumerate(pieces):
        x = ahead_of(here, offset)
        u0_wide[:, pl.ds(pl.multiple_of(x * c, c), c)] = piece[:m]
        rows = pl.ds(pl.multiple_of(x * j, j), j)
        for t in range(n):
            for d in range(RING):
                at = m + (t * RING + d) * j
                tall0[t, rows, d * c : (d + 1) * c] = piece[at : at + j]
    out[...] = sum(nt(tall0[t], v0[t]) for t in range(2))


def gram_01_body(here, tall0, v12, out):
    out[...] = sum(nt(tall0[t], columns(v12, 2 * t)) for t in range(2))


def gram_second_body(here, tall0, pieces, v12, out, tall12, x10_t):
    join_rows(here, pieces, tall12)
    x10_t[...] = tall12[4]
    left = [[split(t) for t in tiles] for tiles in ((tall0[0], tall0[1]), (tall12[0], tall12[1]), (tall12[2], tall12[3]))]
    v1 = [split(columns(v12, 2 * t)) for t in range(2)]
    v2 = [split(columns(v12, 4 + 2 * t)) for t in range(2)]
    for n, (a, v) in enumerate(((1, v1), (0, v2), (1, v2), (2, v2))):
        out[n] = sum(dot3(left[a][t], v[t]) for t in range(2))


def gram_body(here, gram, *outs):
    for offset, out in enumerate(outs):
        c = out.shape[2]
        out[...] = gram[:, :, pl.ds(pl.multiple_of(ahead_of(here, offset) * c, c), c)]


def sum_of(terms):
    return (terms[0][...] + terms[1][...]) + (terms[2][...] + terms[3][...])


def d0_body(here, gram_pieces, m, d0, gram):
    for offset, piece in enumerate(gram_pieces):
        i = piece.shape[1]
        gram[:, pl.ds(pl.multiple_of(behind(here, offset) * i, i), i), :] = piece[...]
    d0[...] = gram[0] - sum_of(m)


def d1_body(here, x10_t, e, e_other, gram, m, m_got, x10, pair, total):
    total[...] = m[...] + m_got[...]
    n = x10.shape[0]
    pair[:n] = gram[1] - nt(x10_t[...], edge(here, e, e_other, 0)) - total[0]
    pair[n:] = x10[...]


def x2_body(here, both_wide, pair_pieces, x10_t, e, e_other, m, packed, x2, pair_wide):
    join_columns(here, pair_pieces, pair_wide)
    n = x10_t.shape[0]
    e1, e2 = split(edge(here, e, e_other, 1)), split(edge(here, e, e_other, 2))
    x20 = -(dot3(split(pair_wide[:n]), e1) + dot3(split(x10_t[...]), e2) + m[2])
    x21 = -(dot3(split(pair_wide[n:]), e1) + dot3(split(both_wide[2 * n :]), e2) + m[1])
    x2[...] = jnp.concatenate([x20, x21], axis=0)
    pack([x2[...]], packed)


def d2_body(here, x2_t_pieces, e, e_other, gram, m, x2, x2_t, new, *outs):
    join_rows(here, x2_t_pieces, x2_t)
    n = gram.shape[1]
    new[n:] = x2[...]
    new[:n] = (
        gram[2]
        - nt(x2_t[0], edge(here, e, e_other, 1))
        - nt(x2_t[1], edge(here, e, e_other, 2))
        - m[3]
    )
    by_offset(here, new, outs)


def corner_body(here, pieces, x2_turned, turned12, _, out):
    band = 2 * here[3] + here[4]
    i = out.shape[2]

    @pl.when(band == 0)
    def _():
        def put(n, at, value):
            out[0, n, :, at] = value

        for n in range(3):
            put_columns(here, pieces, n, functools.partial(put, n))
        out[1, 0] = x2_turned[0]

    @pl.when(band == 1)
    def _():
        out[0, 0] = x2_turned[1]
        out[0, 1] = turned12[4]


def payload_body(here, u0, u1, u2, turned0, turned12, out):
    i = out.shape[2]
    at = pl.multiple_of(here[0] * i, i)

    def put(t, columns_x, value):
        out[2, t, :, columns_x] = value

    for t in range(2):
        for n, ref in enumerate((u0, u1)):
            out[n, t] = ref[pl.ds(t * RING * i + at, i), :]
        put_columns(here, u2, t, functools.partial(put, t))
        out[3, t] = turned0[t]
        out[4, t] = turned12[t]
        out[5, t] = turned12[2 + t]


def final_body(here, pair_wide, both_wide, shared, s_one, s_two, out, done):
    band = 2 * here[3] + here[4]
    i = out.shape[2]
    at = pl.multiple_of(here[0] * i, i)
    done[0] = shared[3, 0, 1]
    done[1] = shared[3, 1, 0]
    done[2] = shared[2, 2, 1]

    @pl.when(band == 0)
    def _():
        out[0, :3] = jnp.zeros((3,) + out.shape[2:], out.dtype)
        out[1, 0] = jnp.zeros(out.shape[2:], out.dtype)
        out[1, 1] = pair_wide[pl.ds(at, i), :]
        out[1, 2] = pair_wide[pl.ds(RING * i + at, i), :]
        for a in range(5):
            out[0, 3 + a] = shared[a // 2, 2, a % 2]
            out[1, 3 + a] = shared[a // 2, 1, a % 2]

    @pl.when(band == 1)
    def _():
        out[0, :2] = jnp.zeros((2,) + out.shape[2:], out.dtype)
        out[0, 2] = both_wide[pl.ds(2 * RING * i + at, i), :]
        for a in range(5):
            out[0, 3 + a] = shared[a // 2, 0, a % 2]

    @pl.when(band >= 2)
    def _():
        for a in range(3):
            out[0, a] = shared[band - 2, 5 - a, 1]
        out[0, 3:] = s_two[...]

    @pl.when(band >= 1)
    def _():
        for a in range(3):
            out[1, a] = shared[band - 1, 5 - a, 0]
        out[1, 3:] = s_one[...]


def local(window, panels, inverse_gram):
    tiles, rows, cols, order = window.shape
    core = lax.axis_index("core")
    zl = lax.axis_index("zl")
    here = jnp.stack([lax.axis_index(a) for a in ("x", "y", "zh", "zl", "core")]).astype(jnp.int32)
    half = order // 2
    quarter = order // RING
    wide_rows = RING * rows
    q = RING * RING
    shards = jnp.transpose(panels, (0, 1, 3, 2))

    v0_zh = ring_gather(shards[0], "zh")
    window_b = jnp.transpose(window, (2, 0, 1, 3))
    s_pieces = ring_gather(window_b.reshape(cols, tiles * rows, order), "x")
    v0_part = call(place_body, [(cols, wide_rows, order)], here, v0_zh)[0]
    v0_pieces = ring_gather(v0_part, "y")

    later = jnp.stack([shards[1, 0], shards[2, 0], shards[2, 1]])
    moved = band_move(later, [(1, 0), (2, 1), (3, 2)])
    low, high = later[:, :, :half], later[:, :, half:]
    edges = jnp.where(core == 0, low, lax.ppermute(high, "core", [(0, 1)]))
    edges = jnp.where(zl == 0, edges, lax.ppermute(edges, "zl", [(0, 1)]))
    batch = call(batch_body, [(11, rows, half)], here, shards[1, 1], moved, edges, wait=(v0_part, s_pieces[1], s_pieces[4]))[0]

    def batch_halves(wait):
        def cut(behind, ahead):
            n, c, s = behind.shape
            return call(halves_body, [(n // 2, c, s), (n - n // 2, c, s)], here, behind, ahead, wait=wait)

        return cut

    batch_zh = ring_gather(batch, "zh", batch_halves((v0_pieces[1], v0_pieces[4], s_pieces[2], s_pieces[3])))
    batch_part = call(place_body, [(11, wide_rows, half)], here, batch_zh, wait=(v0_pieces[2], v0_pieces[3]))[0]

    def scatter(kept, sent):
        kept, sent = call(middle_body, [kept.shape[:1] + kept.shape[2:]] * 2, here, kept, swap(sent, "core"))
        return kept, swap(sent, "zl")

    parts = (RING, 2, cols * rows, quarter)
    block = (cols * wide_rows, quarter)
    wide = (cols * wide_rows, order)
    by_rows = (cols, rows, quarter)

    v0, kept, sent = call(
        first_product_body, [(cols, quarter, order), parts, parts], here, s_pieces, v0_pieces,
        mib=A0_MIB,
    )
    u0, u0_packed = call(column_0_body, [block, (q, rows, cols * wide_rows)], here, *scatter(kept, sent))
    u0_turned, u0_both = call(
        unpack_first_body, [(cols, rows, order), (2 * cols * wide_rows, quarter)], here, over_q(u0_packed), u0
    )
    batch_pieces = ring_gather(batch_part, "y", batch_halves((u0_turned,)))
    u0_pieces = gather_x(u0_both)

    def band_terms(m):
        return (m,) + tuple(
            band_move(m, [(k, k ^ step) for k in range(4)]) for step in (1, 2, 3)
        )

    def band_sum(m):
        m = m + swap(m, "core")
        return m, swap(m, "zl")

    small = (wide_rows, quarter)
    m_00, tall0, u0_wide = call(
        gram_00_body, [small, (cols, wide_rows, order), wide], here, u0_pieces, v0, mib=16
    )

    m_00 = band_terms(m_00)

    v12, e, kept, sent = call(
        later_product_body,
        [(8, quarter, half), (3, quarter, half), parts, parts], here, s_pieces, batch_pieces, wait=m_00[:1], mib=A12_MIB,
    )
    gram_pieces = spread_x(call(gram_body, [(3, rows, quarter)] * RING, here, inverse_gram, wait=(kept,)))
    d0, gram = call(d0_body, [small, (3,) + small], here, gram_pieces, m_00)
    e_other = swap(e, "core")
    last_kept, last_got = scatter(*call(last_product_body, [parts, parts], here, s_pieces, v12, mib=A12_MIB))
    kept, got = scatter(kept, sent)
    u1_d0 = call(
        column_1_body, [((cols + 1) * wide_rows, quarter)], here, kept, got, u0_wide, e, e_other, d0
    )[0]
    m_01 = call(gram_01_body, [small], here, tall0, v12, mib=16)[0]
    both_wide, packed, u2, x10 = call(
        column_2_body,
        [((cols + 1) * wide_rows, order), (q, 2 * rows + rows // 2, cols * wide_rows), block, small], here,
        last_kept, last_got, u0_wide, gather_x(u1_d0), e, e_other, band_terms(m_01),
    )
    turned12 = call(unpack_more_body, [(5, rows, order)], here, over_q(packed))[0]
    kept_tiles = tiles - 3
    shifted = call(shift_body, [(kept_tiles, rows, order)] * 2, here, window_b, wait=(turned12,))
    s_one = band_move(shifted[0], [(0, 1), (1, 2), (2, 3)])
    s_two = band_move(shifted[1], [(0, 2), (1, 3)])
    m_second, _, x10_t = call(
        gram_second_body, [(4, wide_rows, quarter), (5, wide_rows, order), (wide_rows, order)], here,
        tall0, gather_x(turned12), v12, wait=(s_one, s_two), mib=20,
    )
    u2_rows = spread_x(call(by_offset_body, [by_rows] * RING, here, u2, wait=(turned12,)))
    pair, m_second = call(
        d1_body, [(2 * wide_rows, quarter), (4,) + small], here,
        x10_t, e, e_other, gram, *band_sum(m_second), x10, wait=u2_rows[1:],
    )
    x2_packed, x2, pair_wide = call(
        x2_body, [(q, rows, cols * wide_rows), block, (2 * wide_rows, order)], here,
        both_wide, gather_x(pair), x10_t, e, e_other, m_second,
    )
    x2_turned = call(unpack_body, [(cols, rows, order)], here, over_q(x2_packed))[0]
    payload = call(
        payload_body, [(6, cols, rows, order)], here, u0_wide, both_wide, u2_rows, u0_turned, turned12, wait=(pair,)
    )[0]
    shared = lax.all_gather(payload, BAND)

    final, finished = call(
        final_body, [(cols, tiles, rows, order), (3, rows, order)], here, pair_wide, both_wide, shared, s_one, s_two
    )
    _, _, *new = call(
        d2_body, [(cols, wide_rows, order), (3 * wide_rows, quarter)] + [(3, rows, quarter)] * RING, here,
        gather_x(x2_turned), e, e_other, gram, m_second, x2, wait=(final,),
    )
    final = call(
        corner_body, [(cols, tiles, rows, order)], here, spread_x(new), x2_turned, turned12, final,
        alias={RING + 3: 0},
    )[0]
    final = jnp.transpose(final, (1, 2, 0, 3))
    return final, finished


def solution(mesh):
    fine = Mesh(mesh.devices.reshape(RING, RING, RING, 2, 2), ("x", "y", "zh", "zl", "core"))
    rows = ("x", "y", "zh")
    return jax.shard_map(
        local,
        mesh=fine,
        in_specs=(P(None, rows, BAND, None), P(None, BAND, None, rows), P(None, rows, None)),
        out_specs=(P(None, rows, BAND, None), P(None, rows, None)),
        check_vma=False,
    )
```

```python
import functools

import jax
import jax.numpy as jnp
from jax import lax
from jax.experimental import pallas as pl
from jax.experimental.pallas import tpu as pltpu
from jax.sharding import Mesh
from jax.sharding import PartitionSpec as P

RING = 4
BAND = ("zl", "core")
Q = ("y", "zh")
F32 = jnp.float32
MIB = 1024 * 1024
A0_MIB = 16
A12_MIB = 24


def call(body, outs, here, *ins, wait=(), mib=8, alias=None):
    leaves, tree = jax.tree.flatten(ins)
    n, m = len(leaves), len(wait)

    def run(here_ref, *refs):
        body(here_ref, *jax.tree.unflatten(tree, refs[:n]), *refs[n + m :])

    return pl.pallas_call(
        run,
        out_shape=[jax.ShapeDtypeStruct(o, F32) for o in outs],
        in_specs=[pl.BlockSpec(memory_space=pltpu.SMEM)]
        + [pl.BlockSpec(memory_space=pltpu.VMEM)] * n
        + [pl.BlockSpec(memory_space=pl.ANY)] * m,
        out_specs=[pl.BlockSpec(memory_space=pltpu.VMEM)] * len(outs),
        input_output_aliases=alias or {},
        compiler_params=pltpu.CompilerParams(vmem_limit_bytes=mib * MIB),
    )(here, *leaves, *wait)


def split(x):
    high = x.astype(jnp.bfloat16)
    return high, (x - high.astype(F32)).astype(jnp.bfloat16)


def dot3(a, b):
    one = lambda p, q: lax.dot_general(p, q, (((1,), (1,)), ((), ())), preferred_element_type=F32)
    return one(a[0], b[0]) + (one(a[0], b[1]) + one(a[1], b[0]))


def nt(a, b):
    return dot3(split(a), split(b))


def forward(x, axis):
    return lax.ppermute(x, axis, [(i, (i + 1) % RING) for i in range(RING)])


def backward(x, axis):
    return lax.ppermute(x, axis, [(i, (i - 1) % RING) for i in range(RING)])


def swap(x, axis):
    return lax.ppermute(x, axis, [(0, 1), (1, 0)])


def band_move(x, pairs):
    return lax.ppermute(x, BAND, pairs)


def ring_gather(x, axis, halves=None):
    half = x.shape[0] // 2
    behind = forward(x, axis)
    ahead = backward(x, axis)
    low, high = halves(behind, ahead) if halves else (behind[:half], ahead[half:])
    return x, ahead, forward(low, axis), backward(high, axis), behind


def gather_x(x):
    return (x,) + tuple(
        lax.ppermute(x, "x", [((i + offset) % RING, i) for i in range(RING)]) for offset in range(1, RING)
    )


def spread_x(blocks):
    return (blocks[0],) + tuple(
        lax.ppermute(blocks[offset], "x", [(i, (i + offset) % RING) for i in range(RING)])
        for offset in range(1, RING)
    )


def over_q(x):
    return lax.all_to_all(x, Q, 0, 0)


def place(at, pieces, put):
    own, ahead, far_low, far_high, behind = pieces
    c = own.shape[1]
    half = own.shape[0] // 2
    for piece, first, offset in (
        (own, 0, 0), (ahead, 0, 1), (far_low, 0, 2), (far_high, half, 2), (behind, 0, 3)
    ):
        put(piece, first, pl.ds(pl.multiple_of(lax.rem(at + offset, RING) * c, c), c))


def place_body(here, pieces, out):
    def put(piece, first, rows):
        out[first : first + piece.shape[0], rows, :] = piece[...]

    place(here[2], pieces, put)


def batch_body(here, near, moved, edges, out):
    half = near.shape[1] // 2
    for n, tile in enumerate((near[...], moved[0], moved[1], moved[2])):
        out[2 * n] = tile[:, :half]
        out[2 * n + 1] = tile[:, half:]
    out[8:] = edges[...]


def window_product(here, pieces, v, kept, sent):
    total = None
    for b in range(2):
        rows = jnp.concatenate([pieces[0][b], pieces[1][b], pieces[2 + b][0], pieces[4][b]], axis=0)
        term = nt(rows, v[b])
        total = term if total is None else total + term
    core = here[4]
    block = pieces[0].shape[1]
    pair = block // 4
    for offset in range(RING):
        x = ahead_of(here, offset)
        for zl in range(2):
            for c in range(2):
                first = offset * block + (zl * 2 + c) * pair
                part = total[first : first + pair]

                @pl.when(core == c)
                def _():
                    kept[x, zl] = part

                @pl.when(core != c)
                def _():
                    sent[x, zl] = part


def first_product_body(here, s_pieces, v_pieces, v0, kept, sent):
    def put(piece, first, rows):
        v0[first : first + piece.shape[0], rows, :] = piece[...]

    place(here[1], v_pieces, put)
    window_product(here, s_pieces, (v0[0], v0[1]), kept, sent)


def columns(v, first):
    return jnp.concatenate([v[first], v[first + 1]], axis=1)


def later_product_body(here, s_pieces, v_pieces, v12, e, kept, sent):
    n = v12.shape[0]

    def put(piece, first, rows):
        for m in range(piece.shape[0]):
            if first + m < n:
                v12[first + m, rows, :] = piece[m]
            else:
                e[first + m - n, rows, :] = piece[m]

    place(here[1], v_pieces, put)
    window_product(here, s_pieces, (columns(v12, 0), columns(v12, 2)), kept, sent)


def last_product_body(here, s_pieces, v12, kept, sent):
    window_product(here, s_pieces, (columns(v12, 4), columns(v12, 6)), kept, sent)


def halves_body(here, behind, ahead, low, high):
    half = low.shape[0]
    low[...] = behind[:half]
    high[...] = ahead[half:]


def middle_body(here, kept, got, kept2, sent2):
    zl = here[3]
    for z in range(2):
        part = kept[:, z] + got[:, z]

        @pl.when(zl == z)
        def _():
            kept2[...] = part

        @pl.when(zl != z)
        def _():
            sent2[...] = part


def edge(here, mine, other, n):
    first = here[4] == 0
    a, b = mine[n], other[n]
    return jnp.concatenate([jnp.where(first, a, b), jnp.where(first, b, a)], axis=1)


def join_columns(here, pieces, out):
    c = pieces[0].shape[1]
    for offset, piece in enumerate(pieces):
        x = lax.rem(here[0] + offset, RING)
        out[:, pl.ds(pl.multiple_of(x * c, c), c)] = piece[...]


def join_rows(here, pieces, out):
    j = pieces[0].shape[-2]
    for offset, piece in enumerate(pieces):
        x = lax.rem(here[0] + offset, RING)
        rows = pl.ds(pl.multiple_of(x * j, j), j)
        if len(out.shape) == 2:
            out[rows, :] = piece[...]
        else:
            out[:, rows, :] = piece[...]


def blocks_of(kept, got):
    total = -(kept[...] + got[...])
    i = total.shape[1] // 2
    return jnp.concatenate([total[x, t * i : (t + 1) * i] for t in range(2) for x in range(RING)], axis=0)


def pack(blocks, out):
    q = out.shape[0]
    for n, u in enumerate(blocks):
        half = u.shape[0] // 2
        turned = jnp.concatenate([u[:half].T, u[half:].T], axis=1)
        j = turned.shape[0] // q
        out[:, n * j : (n + 1) * j, :] = turned.reshape(q, j, 2 * half)


def ahead_of(here, offset):
    return lax.rem(here[0] + offset, RING)


def behind(here, offset):
    return lax.rem(here[0] + RING - offset, RING)


def by_offset(here, u, outs):
    for offset, out in enumerate(outs):
        t, i, _ = out.shape
        for n in range(t):
            at = pl.multiple_of(n * RING * i + ahead_of(here, offset) * i, i)
            out[n] = u[pl.ds(at, i), :]


def put_columns(here, pieces, n, put):
    for offset, piece in enumerate(pieces):
        c = piece.shape[2]
        put(pl.ds(pl.multiple_of(behind(here, offset) * c, c), c), piece[n])


def column_0_body(here, kept, got, u0, packed):
    u0[...] = blocks_of(kept, got)
    pack([u0[...]], packed)


def column_1_body(here, kept, got, u0_wide, e, e_other, d0, out):
    m = u0_wide.shape[0]
    out[:m] = blocks_of(kept, got) - nt(u0_wide[...], edge(here, e, e_other, 0))
    out[m:] = d0[...]


def column_2_body(here, kept, got, u0_wide, pieces, e, e_other, m, both_wide, packed, u2, x10):
    join_columns(here, pieces, both_wide)
    n = u2.shape[0]
    e0 = edge(here, e, e_other, 0)
    later = blocks_of(kept, got) - nt(both_wide[:n], edge(here, e, e_other, 1))
    u2[...] = later - nt(u0_wide[...], edge(here, e, e_other, 2))
    x10[...] = -(nt(both_wide[n:], e0) + sum_of(m))
    j = x10.shape[1] // packed.shape[0]
    pack([pieces[0][:n], u2[...]], packed.at[:, : 2 * j])
    q = packed.shape[0]
    turned = x10[...].T.reshape(q, j, x10.shape[0])
    packed[:, 2 * j :] = jnp.concatenate([turned[:, : j // 2], turned[:, j // 2 :]], axis=2)


def shift_body(here, window, one, two):
    n = one.shape[0]
    one[...] = window[0, :n]
    two[...] = window[1, :n]


def by_offset_body(here, u, *outs):
    by_offset(here, u, outs)


def unpack_body(here, got, out):
    q, rows, lanes = got.shape
    i = lanes // 8
    j = out.shape[1]
    for n in range(rows // j):
        for t in range(2):
            for x in range(RING):
                at = (t * RING + x) * i
                out[2 * n + t, :, x * q * i : (x + 1) * q * i] = jnp.concatenate(
                    [got[d, n * j : (n + 1) * j, at : at + i] for d in range(q)], axis=1
                )


def unpack_first_body(here, got, u0, turned, out):
    unpack_body(here, got, turned)
    n, j, _ = turned.shape
    m, c = u0.shape
    out[:m] = u0[...]
    for t in range(n):
        for x in range(RING):
            at = m + (t * RING + x) * j
            out[at : at + j] = turned[t, :, x * c : (x + 1) * c]


def unpack_more_body(here, got, out):
    q, _, lanes = got.shape
    i = lanes // 8
    j = out.shape[1]
    for n in range(3):
        rows = slice(n * j, n * j + (j if n < 2 else j // 2))
        for h in range(2):
            for x in range(RING):
                at = (h * RING + x) * i
                part = jnp.concatenate([got[d, rows, at : at + i] for d in range(q)], axis=1)
                columns_x = slice(x * q * i, (x + 1) * q * i)
                if n < 2:
                    out[2 * n + h, :, columns_x] = part
                else:
                    out[4, h * (j // 2) : (h + 1) * (j // 2), columns_x] = part


def gram_00_body(here, pieces, v0, out, tall0, u0_wide):
    n, wide_rows, _ = tall0.shape
    j = wide_rows // RING
    m, c = u0_wide.shape[0], pieces[0].shape[1]
    for offset, piece in enumerate(pieces):
        x = ahead_of(here, offset)
        u0_wide[:, pl.ds(pl.multiple_of(x * c, c), c)] = piece[:m]
        rows = pl.ds(pl.multiple_of(x * j, j), j)
        for t in range(n):
            for d in range(RING):
                at = m + (t * RING + d) * j
                tall0[t, rows, d * c : (d + 1) * c] = piece[at : at + j]
    out[...] = sum(nt(tall0[t], v0[t]) for t in range(2))


def gram_01_body(here, tall0, v12, out):
    out[...] = sum(nt(tall0[t], columns(v12, 2 * t)) for t in range(2))


def gram_second_body(here, tall0, pieces, v12, out, tall12, x10_t):
    join_rows(here, pieces, tall12)
    x10_t[...] = tall12[4]
    left = [[split(t) for t in tiles] for tiles in ((tall0[0], tall0[1]), (tall12[0], tall12[1]), (tall12[2], tall12[3]))]
    v1 = [split(columns(v12, 2 * t)) for t in range(2)]
    v2 = [split(columns(v12, 4 + 2 * t)) for t in range(2)]
    for n, (a, v) in enumerate(((1, v1), (0, v2), (1, v2), (2, v2))):
        out[n] = sum(dot3(left[a][t], v[t]) for t in range(2))


def gram_body(here, gram, *outs):
    for offset, out in enumerate(outs):
        c = out.shape[2]
        out[...] = gram[:, :, pl.ds(pl.multiple_of(ahead_of(here, offset) * c, c), c)]


def sum_of(terms):
    return (terms[0][...] + terms[1][...]) + (terms[2][...] + terms[3][...])


def d0_body(here, gram_pieces, m, d0, gram):
    for offset, piece in enumerate(gram_pieces):
        i = piece.shape[1]
        gram[:, pl.ds(pl.multiple_of(behind(here, offset) * i, i), i), :] = piece[...]
    d0[...] = gram[0] - sum_of(m)


def d1_body(here, x10_t, e, e_other, gram, m, m_got, x10, pair, total):
    total[...] = m[...] + m_got[...]
    n = x10.shape[0]
    pair[:n] = gram[1] - nt(x10_t[...], edge(here, e, e_other, 0)) - total[0]
    pair[n:] = x10[...]


def x2_body(here, both_wide, pair_pieces, x10_t, e, e_other, m, packed, x2, pair_wide):
    join_columns(here, pair_pieces, pair_wide)
    n = x10_t.shape[0]
    e1, e2 = split(edge(here, e, e_other, 1)), split(edge(here, e, e_other, 2))
    x20 = -(dot3(split(pair_wide[:n]), e1) + dot3(split(x10_t[...]), e2) + m[2])
    x21 = -(dot3(split(pair_wide[n:]), e1) + dot3(split(both_wide[2 * n :]), e2) + m[1])
    x2[...] = jnp.concatenate([x20, x21], axis=0)
    pack([x2[...]], packed)


def d2_body(here, x2_t_pieces, e, e_other, gram, m, x2, x2_t, new, *outs):
    join_rows(here, x2_t_pieces, x2_t)
    n = gram.shape[1]
    new[n:] = x2[...]
    new[:n] = (
        gram[2]
        - nt(x2_t[0], edge(here, e, e_other, 1))
        - nt(x2_t[1], edge(here, e, e_other, 2))
        - m[3]
    )
    by_offset(here, new, outs)


def corner_body(here, pieces, x2_turned, turned12, _, out):
    band = 2 * here[3] + here[4]
    i = out.shape[2]

    @pl.when(band == 0)
    def _():
        def put(n, at, value):
            out[0, n, :, at] = value

        for n in range(3):
            put_columns(here, pieces, n, functools.partial(put, n))
        out[1, 0] = x2_turned[0]

    @pl.when(band == 1)
    def _():
        out[0, 0] = x2_turned[1]
        out[0, 1] = turned12[4]


def payload_body(here, u0, u1, u2, turned0, turned12, out):
    i = out.shape[2]
    at = pl.multiple_of(here[0] * i, i)

    def put(t, columns_x, value):
        out[2, t, :, columns_x] = value

    for t in range(2):
        for n, ref in enumerate((u0, u1)):
            out[n, t] = ref[pl.ds(t * RING * i + at, i), :]
        put_columns(here, u2, t, functools.partial(put, t))
        out[3, t] = turned0[t]
        out[4, t] = turned12[t]
        out[5, t] = turned12[2 + t]


def final_body(here, pair_wide, both_wide, shared, s_one, s_two, out, done, sems):
    band = 2 * here[3] + here[4]
    i = out.shape[2]
    at = pl.multiple_of(here[0] * i, i)

    def rows(ref, first):
        return ref.at[pl.ds(pl.multiple_of(first + at, i), i)]

    def move(first, pairs):
        copies = [pltpu.make_async_copy(a, b, sems.at[first + n]) for n, (a, b) in enumerate(pairs)]
        for copy in copies:
            copy.start()
        return copies

    def finish(copies):
        for copy in copies:
            copy.wait()

    ends = move(0, [(shared.at[3, 0, 1], done.at[0]), (shared.at[3, 1, 0], done.at[1]), (shared.at[2, 2, 1], done.at[2])])

    def held(slot, n):
        return [
            (shared.at[0, n], out.at[slot, pl.ds(3, 2)]),
            (shared.at[1, n], out.at[slot, pl.ds(5, 2)]),
            (shared.at[2, n, 0], out.at[slot, 7]),
        ]

    @pl.when(band == 0)
    def _():
        finish(move(3, held(0, 2) + held(1, 1) + [
            (rows(pair_wide, 0), out.at[1, 1]), (rows(pair_wide, RING * i), out.at[1, 2])
        ]))

    @pl.when(band == 1)
    def _():
        finish(move(3, held(0, 0) + [(rows(both_wide, 2 * RING * i), out.at[0, 2])] + [
            (shared.at[0, 5 - a, 0], out.at[1, a]) for a in range(3)
        ] + [(s_one, out.at[1, pl.ds(3, 5)])]))

    @pl.when(band >= 2)
    def _():
        finish(move(3, [(shared.at[band - 2, 5 - a, 1], out.at[0, a]) for a in range(3)] + [
            (s_two, out.at[0, pl.ds(3, 5)])
        ] + [(shared.at[band - 1, 5 - a, 0], out.at[1, a]) for a in range(3)] + [
            (s_one, out.at[1, pl.ds(3, 5)])
        ]))

    finish(ends)


def local(window, panels, inverse_gram):
    tiles, rows, cols, order = window.shape
    core = lax.axis_index("core")
    zl = lax.axis_index("zl")
    here = jnp.stack([lax.axis_index(a) for a in ("x", "y", "zh", "zl", "core")]).astype(jnp.int32)
    half = order // 2
    quarter = order // RING
    wide_rows = RING * rows
    q = RING * RING
    shards = jnp.transpose(panels, (0, 1, 3, 2))

    v0_zh = ring_gather(shards[0], "zh")
    window_b = jnp.transpose(window, (2, 0, 1, 3))
    s_pieces = ring_gather(window_b.reshape(cols, tiles * rows, order), "x")
    v0_part = call(place_body, [(cols, wide_rows, order)], here, v0_zh)[0]
    v0_pieces = ring_gather(v0_part, "y")

    later = jnp.stack([shards[1, 0], shards[2, 0], shards[2, 1]])
    moved = band_move(later, [(1, 0), (2, 1), (3, 2)])
    low, high = later[:, :, :half], later[:, :, half:]
    edges = jnp.where(core == 0, low, lax.ppermute(high, "core", [(0, 1)]))
    edges = jnp.where(zl == 0, edges, lax.ppermute(edges, "zl", [(0, 1)]))
    batch = call(batch_body, [(11, rows, half)], here, shards[1, 1], moved, edges, wait=(v0_part, s_pieces[1], s_pieces[4]))[0]

    def batch_halves(wait):
        def cut(behind, ahead):
            n, c, s = behind.shape
            return call(halves_body, [(n // 2, c, s), (n - n // 2, c, s)], here, behind, ahead, wait=wait)

        return cut

    batch_zh = ring_gather(batch, "zh", batch_halves((v0_pieces[1], v0_pieces[4], s_pieces[2], s_pieces[3])))
    batch_part = call(place_body, [(11, wide_rows, half)], here, batch_zh, wait=(v0_pieces[2], v0_pieces[3]))[0]

    def scatter(kept, sent):
        kept, sent = call(middle_body, [kept.shape[:1] + kept.shape[2:]] * 2, here, kept, swap(sent, "core"))
        return kept, swap(sent, "zl")

    parts = (RING, 2, cols * rows, quarter)
    block = (cols * wide_rows, quarter)
    wide = (cols * wide_rows, order)
    by_rows = (cols, rows, quarter)

    v0, kept, sent = call(
        first_product_body, [(cols, quarter, order), parts, parts], here, s_pieces, v0_pieces,
        mib=A0_MIB,
    )
    u0, u0_packed = call(column_0_body, [block, (q, rows, cols * wide_rows)], here, *scatter(kept, sent))
    u0_turned, u0_both = call(
        unpack_first_body, [(cols, rows, order), (2 * cols * wide_rows, quarter)], here, over_q(u0_packed), u0
    )
    batch_pieces = ring_gather(batch_part, "y", batch_halves((u0_turned,)))
    u0_pieces = gather_x(u0_both)

    def band_terms(m):
        return (m,) + tuple(
            band_move(m, [(k, k ^ step) for k in range(4)]) for step in (1, 2, 3)
        )

    def band_sum(m):
        m = m + swap(m, "core")
        return m, swap(m, "zl")

    small = (wide_rows, quarter)
    m_00, tall0, u0_wide = call(
        gram_00_body, [small, (cols, wide_rows, order), wide], here, u0_pieces, v0, mib=16
    )

    m_00 = band_terms(m_00)

    v12, e, kept, sent = call(
        later_product_body,
        [(8, quarter, half), (3, quarter, half), parts, parts], here, s_pieces, batch_pieces, wait=m_00[:1], mib=A12_MIB,
    )
    gram_pieces = spread_x(call(gram_body, [(3, rows, quarter)] * RING, here, inverse_gram, wait=(kept,)))
    d0, gram = call(d0_body, [small, (3,) + small], here, gram_pieces, m_00)
    e_other = swap(e, "core")
    last_kept, last_got = scatter(*call(last_product_body, [parts, parts], here, s_pieces, v12, mib=A12_MIB))
    kept, got = scatter(kept, sent)
    u1_d0 = call(
        column_1_body, [((cols + 1) * wide_rows, quarter)], here, kept, got, u0_wide, e, e_other, d0
    )[0]
    m_01 = call(gram_01_body, [small], here, tall0, v12, mib=16)[0]
    both_wide, packed, u2, x10 = call(
        column_2_body,
        [((cols + 1) * wide_rows, order), (q, 2 * rows + rows // 2, cols * wide_rows), block, small], here,
        last_kept, last_got, u0_wide, gather_x(u1_d0), e, e_other, band_terms(m_01),
    )
    turned12 = call(unpack_more_body, [(5, rows, order)], here, over_q(packed))[0]
    kept_tiles = tiles - 3
    shifted = call(shift_body, [(kept_tiles, rows, order)] * 2, here, window_b, wait=(turned12,))
    s_one = band_move(shifted[0], [(0, 1), (1, 2), (2, 3)])
    s_two = band_move(shifted[1], [(0, 2), (1, 3)])
    m_second, _, x10_t = call(
        gram_second_body, [(4, wide_rows, quarter), (5, wide_rows, order), (wide_rows, order)], here,
        tall0, gather_x(turned12), v12, wait=(s_one, s_two), mib=20,
    )
    u2_rows = spread_x(call(by_offset_body, [by_rows] * RING, here, u2, wait=(turned12,)))
    pair, m_second = call(
        d1_body, [(2 * wide_rows, quarter), (4,) + small], here,
        x10_t, e, e_other, gram, *band_sum(m_second), x10, wait=u2_rows[1:],
    )
    x2_packed, x2, pair_wide = call(
        x2_body, [(q, rows, cols * wide_rows), block, (2 * wide_rows, order)], here,
        both_wide, gather_x(pair), x10_t, e, e_other, m_second,
    )
    x2_turned = call(unpack_body, [(cols, rows, order)], here, over_q(x2_packed))[0]
    payload = call(
        payload_body, [(6, cols, rows, order)], here, u0_wide, both_wide, u2_rows, u0_turned, turned12, wait=(pair,)
    )[0]
    shared = lax.all_gather(payload, BAND)

    final, finished = pl.pallas_call(
        final_body,
        out_shape=[jax.ShapeDtypeStruct(o, F32) for o in ((cols, tiles, rows, order), (3, rows, order))],
        in_specs=[pl.BlockSpec(memory_space=pltpu.SMEM)] + [pl.BlockSpec(memory_space=pl.ANY)] * 5,
        out_specs=[pl.BlockSpec(memory_space=pltpu.VMEM)] * 2,
        scratch_shapes=[pltpu.SemaphoreType.DMA((11,))],
        compiler_params=pltpu.CompilerParams(vmem_limit_bytes=8 * MIB),
    )(here, pair_wide, both_wide, shared, s_one, s_two)
    _, _, *new = call(
        d2_body, [(cols, wide_rows, order), (3 * wide_rows, quarter)] + [(3, rows, quarter)] * RING, here,
        gather_x(x2_turned), e, e_other, gram, m_second, x2,
    )
    final = call(
        corner_body, [(cols, tiles, rows, order)], here, spread_x(new), x2_turned, turned12, final,
        alias={RING + 3: 0},
    )[0]
    final = jnp.transpose(final, (1, 2, 0, 3))
    return final, finished


def solution(mesh):
    fine = Mesh(mesh.devices.reshape(RING, RING, RING, 2, 2), ("x", "y", "zh", "zl", "core"))
    rows = ("x", "y", "zh")
    return jax.shard_map(
        local,
        mesh=fine,
        in_specs=(P(None, rows, BAND, None), P(None, BAND, None, rows), P(None, rows, None)),
        out_specs=(P(None, rows, BAND, None), P(None, rows, None)),
        check_vma=False,
    )
```

```python
import functools

import jax
import jax.numpy as jnp
from jax import lax
from jax.experimental import pallas as pl
from jax.experimental.pallas import tpu as pltpu
from jax.sharding import Mesh
from jax.sharding import PartitionSpec as P

RING = 4
BAND = ("zl", "core")
Q = ("y", "zh")
F32 = jnp.float32
MIB = 1024 * 1024
A0_MIB = 16
A12_MIB = 24


def call(body, outs, here, *ins, wait=(), mib=8, alias=None):
    leaves, tree = jax.tree.flatten(ins)
    n, m = len(leaves), len(wait)

    def run(here_ref, *refs):
        body(here_ref, *jax.tree.unflatten(tree, refs[:n]), *refs[n + m :])

    return pl.pallas_call(
        run,
        out_shape=[jax.ShapeDtypeStruct(o, F32) for o in outs],
        in_specs=[pl.BlockSpec(memory_space=pltpu.SMEM)]
        + [pl.BlockSpec(memory_space=pltpu.VMEM)] * n
        + [pl.BlockSpec(memory_space=pl.ANY)] * m,
        out_specs=[pl.BlockSpec(memory_space=pltpu.VMEM)] * len(outs),
        input_output_aliases=alias or {},
        compiler_params=pltpu.CompilerParams(vmem_limit_bytes=mib * MIB),
    )(here, *leaves, *wait)


def split(x):
    high = x.astype(jnp.bfloat16)
    return high, (x - high.astype(F32)).astype(jnp.bfloat16)


def dot3(a, b):
    one = lambda p, q: lax.dot_general(p, q, (((1,), (1,)), ((), ())), preferred_element_type=F32)
    return one(a[0], b[0]) + (one(a[0], b[1]) + one(a[1], b[0]))


def nt(a, b):
    return dot3(split(a), split(b))


def forward(x, axis):
    return lax.ppermute(x, axis, [(i, (i + 1) % RING) for i in range(RING)])


def backward(x, axis):
    return lax.ppermute(x, axis, [(i, (i - 1) % RING) for i in range(RING)])


def swap(x, axis):
    return lax.ppermute(x, axis, [(0, 1), (1, 0)])


def band_move(x, pairs):
    return lax.ppermute(x, BAND, pairs)


def ring_gather(x, axis, halves=None):
    half = x.shape[0] // 2
    behind = forward(x, axis)
    ahead = backward(x, axis)
    low, high = halves(behind, ahead) if halves else (behind[:half], ahead[half:])
    return x, ahead, forward(low, axis), backward(high, axis), behind


def gather_x(x):
    return (x,) + tuple(
        lax.ppermute(x, "x", [((i + offset) % RING, i) for i in range(RING)]) for offset in range(1, RING)
    )


def spread_x(blocks):
    return (blocks[0],) + tuple(
        lax.ppermute(blocks[offset], "x", [(i, (i + offset) % RING) for i in range(RING)])
        for offset in range(1, RING)
    )


def over_q(x):
    return lax.all_to_all(x, Q, 0, 0)


def place(at, pieces, put):
    own, ahead, far_low, far_high, behind = pieces
    c = own.shape[1]
    half = own.shape[0] // 2
    for piece, first, offset in (
        (own, 0, 0), (ahead, 0, 1), (far_low, 0, 2), (far_high, half, 2), (behind, 0, 3)
    ):
        put(piece, first, pl.ds(pl.multiple_of(lax.rem(at + offset, RING) * c, c), c))


def place_body(here, pieces, out):
    def put(piece, first, rows):
        out[first : first + piece.shape[0], rows, :] = piece[...]

    place(here[2], pieces, put)


def batch_body(here, near, moved, edges, out):
    half = near.shape[1] // 2
    for n, tile in enumerate((near[...], moved[0], moved[1], moved[2])):
        out[2 * n] = tile[:, :half]
        out[2 * n + 1] = tile[:, half:]
    out[8:] = edges[...]


def window_product(here, pieces, v, kept, sent):
    total = None
    for b in range(2):
        rows = jnp.concatenate([pieces[0][b], pieces[1][b], pieces[2 + b][0], pieces[4][b]], axis=0)
        term = nt(rows, v[b])
        total = term if total is None else total + term
    core = here[4]
    block = pieces[0].shape[1]
    pair = block // 4
    for offset in range(RING):
        x = ahead_of(here, offset)
        for zl in range(2):
            for c in range(2):
                first = offset * block + (zl * 2 + c) * pair
                part = total[first : first + pair]

                @pl.when(core == c)
                def _():
                    kept[x, zl] = part

                @pl.when(core != c)
                def _():
                    sent[x, zl] = part


def first_product_body(here, s_pieces, v_pieces, v0, kept, sent):
    def put(piece, first, rows):
        v0[first : first + piece.shape[0], rows, :] = piece[...]

    place(here[1], v_pieces, put)
    window_product(here, s_pieces, (v0[0], v0[1]), kept, sent)


def columns(v, first):
    return jnp.concatenate([v[first], v[first + 1]], axis=1)


def later_product_body(here, s_pieces, v_pieces, v12, e, kept, sent):
    n = v12.shape[0]

    def put(piece, first, rows):
        for m in range(piece.shape[0]):
            if first + m < n:
                v12[first + m, rows, :] = piece[m]
            else:
                e[first + m - n, rows, :] = piece[m]

    place(here[1], v_pieces, put)
    window_product(here, s_pieces, (columns(v12, 0), columns(v12, 2)), kept, sent)


def last_product_body(here, s_pieces, v12, kept, sent):
    window_product(here, s_pieces, (columns(v12, 4), columns(v12, 6)), kept, sent)


def halves_body(here, behind, ahead, low, high):
    half = low.shape[0]
    low[...] = behind[:half]
    high[...] = ahead[half:]


def middle_body(here, kept, got, kept2, sent2):
    zl = here[3]
    for z in range(2):
        part = kept[:, z] + got[:, z]

        @pl.when(zl == z)
        def _():
            kept2[...] = part

        @pl.when(zl != z)
        def _():
            sent2[...] = part


def edge(here, mine, other, n):
    first = here[4] == 0
    a, b = mine[n], other[n]
    return jnp.concatenate([jnp.where(first, a, b), jnp.where(first, b, a)], axis=1)


def join_columns(here, pieces, out):
    c = pieces[0].shape[1]
    for offset, piece in enumerate(pieces):
        x = lax.rem(here[0] + offset, RING)
        out[:, pl.ds(pl.multiple_of(x * c, c), c)] = piece[...]


def join_rows(here, pieces, out):
    j = pieces[0].shape[-2]
    for offset, piece in enumerate(pieces):
        x = lax.rem(here[0] + offset, RING)
        rows = pl.ds(pl.multiple_of(x * j, j), j)
        if len(out.shape) == 2:
            out[rows, :] = piece[...]
        else:
            out[:, rows, :] = piece[...]


def blocks_of(kept, got):
    total = -(kept[...] + got[...])
    i = total.shape[1] // 2
    return jnp.concatenate([total[x, t * i : (t + 1) * i] for t in range(2) for x in range(RING)], axis=0)


def pack(blocks, out):
    q = out.shape[0]
    for n, u in enumerate(blocks):
        half = u.shape[0] // 2
        turned = jnp.concatenate([u[:half].T, u[half:].T], axis=1)
        j = turned.shape[0] // q
        out[:, n * j : (n + 1) * j, :] = turned.reshape(q, j, 2 * half)


def ahead_of(here, offset):
    return lax.rem(here[0] + offset, RING)


def behind(here, offset):
    return lax.rem(here[0] + RING - offset, RING)


def by_offset(here, u, outs):
    for offset, out in enumerate(outs):
        t, i, _ = out.shape
        for n in range(t):
            at = pl.multiple_of(n * RING * i + ahead_of(here, offset) * i, i)
            out[n] = u[pl.ds(at, i), :]


def put_columns(here, pieces, n, put):
    for offset, piece in enumerate(pieces):
        c = piece.shape[2]
        put(pl.ds(pl.multiple_of(behind(here, offset) * c, c), c), piece[n])


def column_0_body(here, kept, got, u0, packed):
    u0[...] = blocks_of(kept, got)
    pack([u0[...]], packed)


def column_1_body(here, kept, got, u0_wide, e, e_other, d0, out):
    m = u0_wide.shape[0]
    out[:m] = blocks_of(kept, got) - nt(u0_wide[...], edge(here, e, e_other, 0))
    out[m:] = d0[...]


def column_2_body(here, kept, got, u0_wide, pieces, e, e_other, m, both_wide, packed, u2, x10):
    join_columns(here, pieces, both_wide)
    n = u2.shape[0]
    e0 = edge(here, e, e_other, 0)
    later = blocks_of(kept, got) - nt(both_wide[:n], edge(here, e, e_other, 1))
    u2[...] = later - nt(u0_wide[...], edge(here, e, e_other, 2))
    x10[...] = -(nt(both_wide[n:], e0) + sum_of(m))
    j = x10.shape[1] // packed.shape[0]
    pack([pieces[0][:n], u2[...]], packed.at[:, : 2 * j])
    q = packed.shape[0]
    turned = x10[...].T.reshape(q, j, x10.shape[0])
    packed[:, 2 * j :] = jnp.concatenate([turned[:, : j // 2], turned[:, j // 2 :]], axis=2)


def shift_body(here, window, one, two):
    n = one.shape[0]
    one[...] = window[0, :n]
    two[...] = window[1, :n]


def by_offset_body(here, u, *outs):
    by_offset(here, u, outs)


def unpack_body(here, got, out):
    q, rows, lanes = got.shape
    i = lanes // 8
    j = out.shape[1]
    for n in range(rows // j):
        for t in range(2):
            for x in range(RING):
                at = (t * RING + x) * i
                out[2 * n + t, :, x * q * i : (x + 1) * q * i] = jnp.concatenate(
                    [got[d, n * j : (n + 1) * j, at : at + i] for d in range(q)], axis=1
                )


def unpack_first_body(here, got, u0, turned, out):
    unpack_body(here, got, turned)
    n, j, _ = turned.shape
    m, c = u0.shape
    out[:m] = u0[...]
    for t in range(n):
        for x in range(RING):
            at = m + (t * RING + x) * j
            out[at : at + j] = turned[t, :, x * c : (x + 1) * c]


def unpack_more_body(here, got, out):
    q, _, lanes = got.shape
    i = lanes // 8
    j = out.shape[1]
    for n in range(3):
        rows = slice(n * j, n * j + (j if n < 2 else j // 2))
        for h in range(2):
            for x in range(RING):
                at = (h * RING + x) * i
                part = jnp.concatenate([got[d, rows, at : at + i] for d in range(q)], axis=1)
                columns_x = slice(x * q * i, (x + 1) * q * i)
                if n < 2:
                    out[2 * n + h, :, columns_x] = part
                else:
                    out[4, h * (j // 2) : (h + 1) * (j // 2), columns_x] = part


def gram_00_body(here, pieces, v0, out, tall0, u0_wide):
    n, wide_rows, _ = tall0.shape
    j = wide_rows // RING
    m, c = u0_wide.shape[0], pieces[0].shape[1]
    for offset, piece in enumerate(pieces):
        x = ahead_of(here, offset)
        u0_wide[:, pl.ds(pl.multiple_of(x * c, c), c)] = piece[:m]
        rows = pl.ds(pl.multiple_of(x * j, j), j)
        for t in range(n):
            for d in range(RING):
                at = m + (t * RING + d) * j
                tall0[t, rows, d * c : (d + 1) * c] = piece[at : at + j]
    out[...] = sum(nt(tall0[t], v0[t]) for t in range(2))


def gram_01_body(here, tall0, v12, out):
    out[...] = sum(nt(tall0[t], columns(v12, 2 * t)) for t in range(2))


def gram_second_body(here, tall0, pieces, v12, m_11, out, tall12, x10_t):
    join_rows(here, pieces, tall12)
    x10_t[...] = tall12[4]
    left = [[split(t) for t in tiles] for tiles in ((tall0[0], tall0[1]), (tall12[0], tall12[1]), (tall12[2], tall12[3]))]
    v1 = [split(columns(v12, 2 * t)) for t in range(2)]
    v2 = [split(columns(v12, 4 + 2 * t)) for t in range(2)]
    m_11[...] = sum(dot3(left[1][t], v1[t]) for t in range(2))
    for n, (a, v) in enumerate(((0, v2), (1, v2), (2, v2))):
        out[n] = sum(dot3(left[a][t], v[t]) for t in range(2))


def gram_body(here, gram, *outs):
    for offset, out in enumerate(outs):
        c = out.shape[2]
        out[...] = gram[:, :, pl.ds(pl.multiple_of(ahead_of(here, offset) * c, c), c)]


def sum_of(terms):
    return (terms[0][...] + terms[1][...]) + (terms[2][...] + terms[3][...])


def d0_body(here, gram_pieces, m, d0, gram):
    for offset, piece in enumerate(gram_pieces):
        i = piece.shape[1]
        gram[:, pl.ds(pl.multiple_of(behind(here, offset) * i, i), i), :] = piece[...]
    d0[...] = gram[0] - sum_of(m)


def d1_body(here, x10_t, e, e_other, gram, m, x10, pair):
    n = x10.shape[0]
    pair[:n] = gram[1] - nt(x10_t[...], edge(here, e, e_other, 0)) - sum_of(m)
    pair[n:] = x10[...]


def x2_body(here, both_wide, pair_pieces, x10_t, e, e_other, m, m_got, packed, x2, pair_wide):
    join_columns(here, pair_pieces, pair_wide)
    n = x10_t.shape[0]
    e1, e2 = split(edge(here, e, e_other, 1)), split(edge(here, e, e_other, 2))
    x20 = -(dot3(split(pair_wide[:n]), e1) + dot3(split(x10_t[...]), e2) + (m[1] + m_got[1]))
    x21 = -(dot3(split(pair_wide[n:]), e1) + dot3(split(both_wide[2 * n :]), e2) + (m[0] + m_got[0]))
    x2[...] = jnp.concatenate([x20, x21], axis=0)
    pack([x2[...]], packed)


def d2_body(here, x2_t_pieces, e, e_other, gram, m, m_got, x2, x2_t, new, *outs):
    join_rows(here, x2_t_pieces, x2_t)
    n = gram.shape[1]
    new[n:] = x2[...]
    new[:n] = (
        gram[2]
        - nt(x2_t[0], edge(here, e, e_other, 1))
        - nt(x2_t[1], edge(here, e, e_other, 2))
        - (m[2] + m_got[2])
    )
    by_offset(here, new, outs)


def corner_body(here, pieces, x2_turned, turned12, _, out):
    band = 2 * here[3] + here[4]
    i = out.shape[2]

    @pl.when(band == 0)
    def _():
        def put(n, at, value):
            out[0, n, :, at] = value

        for n in range(3):
            put_columns(here, pieces, n, functools.partial(put, n))
        out[1, 0] = x2_turned[0]

    @pl.when(band == 1)
    def _():
        out[0, 0] = x2_turned[1]
        out[0, 1] = turned12[4]


def payload_body(here, u0, u1, u2, turned0, turned12, out):
    i = out.shape[2]
    at = pl.multiple_of(here[0] * i, i)

    def put(t, columns_x, value):
        out[2, t, :, columns_x] = value

    for t in range(2):
        for n, ref in enumerate((u0, u1)):
            out[n, t] = ref[pl.ds(t * RING * i + at, i), :]
        put_columns(here, u2, t, functools.partial(put, t))
        out[3, t] = turned0[t]
        out[4, t] = turned12[t]
        out[5, t] = turned12[2 + t]


def final_body(here, pair_wide, both_wide, shared, s_one, s_two, out, done):
    band = 2 * here[3] + here[4]
    i = out.shape[2]
    at = pl.multiple_of(here[0] * i, i)
    done[0] = shared[3, 0, 1]
    done[1] = shared[3, 1, 0]
    done[2] = shared[2, 2, 1]

    @pl.when(band == 0)
    def _():
        out[0, :3] = jnp.zeros((3,) + out.shape[2:], out.dtype)
        out[1, 0] = jnp.zeros(out.shape[2:], out.dtype)
        out[1, 1] = pair_wide[pl.ds(at, i), :]
        out[1, 2] = pair_wide[pl.ds(RING * i + at, i), :]
        for a in range(5):
            out[0, 3 + a] = shared[a // 2, 2, a % 2]
            out[1, 3 + a] = shared[a // 2, 1, a % 2]

    @pl.when(band == 1)
    def _():
        out[0, :2] = jnp.zeros((2,) + out.shape[2:], out.dtype)
        out[0, 2] = both_wide[pl.ds(2 * RING * i + at, i), :]
        for a in range(5):
            out[0, 3 + a] = shared[a // 2, 0, a % 2]

    @pl.when(band >= 2)
    def _():
        for a in range(3):
            out[0, a] = shared[band - 2, 5 - a, 1]
        out[0, 3:] = s_two[...]

    @pl.when(band >= 1)
    def _():
        for a in range(3):
            out[1, a] = shared[band - 1, 5 - a, 0]
        out[1, 3:] = s_one[...]


def local(window, panels, inverse_gram):
    tiles, rows, cols, order = window.shape
    core = lax.axis_index("core")
    zl = lax.axis_index("zl")
    here = jnp.stack([lax.axis_index(a) for a in ("x", "y", "zh", "zl", "core")]).astype(jnp.int32)
    half = order // 2
    quarter = order // RING
    wide_rows = RING * rows
    q = RING * RING
    shards = jnp.transpose(panels, (0, 1, 3, 2))

    v0_zh = ring_gather(shards[0], "zh")
    window_b = jnp.transpose(window, (2, 0, 1, 3))
    s_pieces = ring_gather(window_b.reshape(cols, tiles * rows, order), "x")
    v0_part = call(place_body, [(cols, wide_rows, order)], here, v0_zh)[0]
    v0_pieces = ring_gather(v0_part, "y")

    later = jnp.stack([shards[1, 0], shards[2, 0], shards[2, 1]])
    moved = band_move(later, [(1, 0), (2, 1), (3, 2)])
    low, high = later[:, :, :half], later[:, :, half:]
    edges = jnp.where(core == 0, low, lax.ppermute(high, "core", [(0, 1)]))
    edges = jnp.where(zl == 0, edges, lax.ppermute(edges, "zl", [(0, 1)]))
    batch = call(batch_body, [(11, rows, half)], here, shards[1, 1], moved, edges, wait=(v0_part, s_pieces[1], s_pieces[4]))[0]

    def batch_halves(wait):
        def cut(behind, ahead):
            n, c, s = behind.shape
            return call(halves_body, [(n // 2, c, s), (n - n // 2, c, s)], here, behind, ahead, wait=wait)

        return cut

    batch_zh = ring_gather(batch, "zh", batch_halves((v0_pieces[1], v0_pieces[4], s_pieces[2], s_pieces[3])))
    batch_part = call(place_body, [(11, wide_rows, half)], here, batch_zh, wait=(v0_pieces[2], v0_pieces[3]))[0]

    def scatter(kept, sent):
        kept, sent = call(middle_body, [kept.shape[:1] + kept.shape[2:]] * 2, here, kept, swap(sent, "core"))
        return kept, swap(sent, "zl")

    parts = (RING, 2, cols * rows, quarter)
    block = (cols * wide_rows, quarter)
    wide = (cols * wide_rows, order)
    by_rows = (cols, rows, quarter)

    v0, kept, sent = call(
        first_product_body, [(cols, quarter, order), parts, parts], here, s_pieces, v0_pieces,
        mib=A0_MIB,
    )
    u0, u0_packed = call(column_0_body, [block, (q, rows, cols * wide_rows)], here, *scatter(kept, sent))
    u0_turned, u0_both = call(
        unpack_first_body, [(cols, rows, order), (2 * cols * wide_rows, quarter)], here, over_q(u0_packed), u0
    )
    batch_pieces = ring_gather(batch_part, "y", batch_halves((u0_turned,)))
    u0_pieces = gather_x(u0_both)

    def band_terms(m):
        return (m,) + tuple(
            band_move(m, [(k, k ^ step) for k in range(4)]) for step in (1, 2, 3)
        )

    def band_sum(m):
        m = m + swap(m, "core")
        return m, swap(m, "zl")

    small = (wide_rows, quarter)
    m_00, tall0, u0_wide = call(
        gram_00_body, [small, (cols, wide_rows, order), wide], here, u0_pieces, v0, mib=16
    )

    m_00 = band_terms(m_00)

    v12, e, kept, sent = call(
        later_product_body,
        [(8, quarter, half), (3, quarter, half), parts, parts], here, s_pieces, batch_pieces, wait=m_00[:1], mib=A12_MIB,
    )
    gram_pieces = spread_x(call(gram_body, [(3, rows, quarter)] * RING, here, inverse_gram, wait=(kept,)))
    d0, gram = call(d0_body, [small, (3,) + small], here, gram_pieces, m_00)
    e_other = swap(e, "core")
    last_kept, last_got = scatter(*call(last_product_body, [parts, parts], here, s_pieces, v12, mib=A12_MIB))
    kept, got = scatter(kept, sent)
    u1_d0 = call(
        column_1_body, [((cols + 1) * wide_rows, quarter)], here, kept, got, u0_wide, e, e_other, d0
    )[0]
    m_01 = call(gram_01_body, [small], here, tall0, v12, mib=16)[0]
    both_wide, packed, u2, x10 = call(
        column_2_body,
        [((cols + 1) * wide_rows, order), (q, 2 * rows + rows // 2, cols * wide_rows), block, small], here,
        last_kept, last_got, u0_wide, gather_x(u1_d0), e, e_other, band_terms(m_01),
    )
    turned12 = call(unpack_more_body, [(5, rows, order)], here, over_q(packed))[0]
    kept_tiles = tiles - 3
    shifted = call(shift_body, [(kept_tiles, rows, order)] * 2, here, window_b, wait=(turned12,))
    s_one = band_move(shifted[0], [(0, 1), (1, 2), (2, 3)])
    s_two = band_move(shifted[1], [(0, 2), (1, 3)])
    m_11, m_second, _, x10_t = call(
        gram_second_body, [small, (3, wide_rows, quarter), (5, wide_rows, order), (wide_rows, order)], here,
        tall0, gather_x(turned12), v12, wait=(s_one, s_two), mib=20,
    )
    u2_rows = spread_x(call(by_offset_body, [by_rows] * RING, here, u2, wait=(turned12,)))
    pair = call(
        d1_body, [(2 * wide_rows, quarter)], here, x10_t, e, e_other, gram, band_terms(m_11), x10
    )[0]
    m_second = band_sum(m_second)
    x2_packed, x2, pair_wide = call(
        x2_body, [(q, rows, cols * wide_rows), block, (2 * wide_rows, order)], here,
        both_wide, gather_x(pair), x10_t, e, e_other, *m_second,
    )
    x2_turned = call(unpack_body, [(cols, rows, order)], here, over_q(x2_packed))[0]
    payload = call(
        payload_body, [(6, cols, rows, order)], here, u0_wide, both_wide, u2_rows, u0_turned, turned12, wait=(pair,)
    )[0]
    shared = lax.all_gather(payload, BAND)

    final, finished = call(
        final_body, [(cols, tiles, rows, order), (3, rows, order)], here, pair_wide, both_wide, shared, s_one, s_two
    )
    _, _, *new = call(
        d2_body, [(cols, wide_rows, order), (3 * wide_rows, quarter)] + [(3, rows, quarter)] * RING, here,
        gather_x(x2_turned), e, e_other, gram, *m_second, x2,
    )
    final = call(
        corner_body, [(cols, tiles, rows, order)], here, spread_x(new), x2_turned, turned12, final,
        alias={RING + 3: 0},
    )[0]
    final = jnp.transpose(final, (1, 2, 0, 3))
    return final, finished


def solution(mesh):
    fine = Mesh(mesh.devices.reshape(RING, RING, RING, 2, 2), ("x", "y", "zh", "zl", "core"))
    rows = ("x", "y", "zh")
    return jax.shard_map(
        local,
        mesh=fine,
        in_specs=(P(None, rows, BAND, None), P(None, BAND, None, rows), P(None, rows, None)),
        out_specs=(P(None, rows, BAND, None), P(None, rows, None)),
        check_vma=False,
    )
```
